512 devices in a mesh: section: 16 (over z, core), tensor: 16 (over x, y_lo), dp: 2 (over y_hi).
Axes of the slice: x: 4, y: 8 (y_hi: 2, y_lo: 4; y = y_hi * 4 + y_lo), z: 8, core: 2. Of those that a mesh axis runs over, the one named last changes fastest.
Arguments:
- section_input: bfloat16 [16, 256, 4096], P('section', 'dp', 'tensor'), parts along dimension 1, may hold values from -6 to 6
- stash_pool: bfloat16 [16, 2, 256, 4096], P('section', None, 'dp', 'tensor'), parts along dimension 2, may hold values from -6 to 6
- reload_slot: int32 [16], P('section'), may hold values from 0 to 1
- cotangent: bfloat16 [16, 256, 4096], P('section', 'dp', 'tensor'), parts along dimension 1, may hold values from -6 to 6
- norm_gain: float32 [16, 4096], P('section', 'tensor'), may hold values from 0.5 to 6
- query_weight: bfloat16 [16, 4096, 4096], P('section', None, 'tensor'), may hold values from -0.09375 to 0.09375
- kv_weight: bfloat16 [16, 4096, 1024], P('section', 'tensor'), may hold values from -0.09375 to 0.09375
- out_weight: bfloat16 [16, 4096, 4096], P('section', 'tensor'), may hold values from -0.09375 to 0.09375
Outputs:
- next_input: bfloat16 [16, 256, 4096], P('section', 'dp', 'tensor'), parts along dimension 1
- received_stash: bfloat16 [16, 256, 4096], P('section', 'dp', 'tensor'), parts along dimension 1
- input_grad: bfloat16 [16, 256, 4096], P('section', 'dp', 'tensor'), parts along dimension 1
The draws below stay inside these ranges and needn't reach their ends.
There are 2 independent parts, one for each index of `dp`. The reference program is written for one: setup_inputs(seed, part) draws one part's arguments, and reference() takes and returns one part's arrays. A program takes and returns all parts, laid end to end along the dimension named above; an argument that names none is the same for every part. Nothing has to cross between parts.
All inputs are finite; a program needn't handle non-finite values.
Results may differ from the reference program's by a relative error of at most 0.024.
The reference program's roundings to bfloat16 on the way count: a program that leaves them out, or rounds other values in their place, can miss the bound.
Values may be sent and summed in bfloat16 or wider, within the bound.
No kernel may reach another device: no remote copies, remote signals or barrier semaphores. Data moves between devices by JAX's collectives and lax.ppermute only.
A program may use at most 64 MiB of HBM per device.

```python
import jax
import jax.numpy as jnp
from jax import lax

D = 4096
HEADS = 32
KVH = 4
HD = 128
TOK = 128
SLOTS = 2
SECTIONS = 16


def draw_norm_gain(key, part):
    key = jax.random.fold_in(key, 11)
    return jnp.clip(1.0 + 0.1 * jax.random.normal(key, (SECTIONS, D), jnp.float32), 0.5, 1.5)


def set_ends(entries, stream_key, least, top_value):
    longest = entries.shape.index(max(entries.shape))
    spots = []
    for shift in (0, 1):
        where = [jax.random.randint(jax.random.fold_in(stream_key, axis), (), 0, length) for axis, length in enumerate(entries.shape)]
        where[longest] = (where[longest] + shift) % entries.shape[longest]
        spots.append(tuple(where))
    return entries.at[spots[0]].set(least).at[spots[1]].set(top_value)


def shard_levels(stream_key, extent, split, least, top_value):
    factor_of = 1.0
    for position, parts in split:
        heights = jax.random.uniform(jax.random.fold_in(jax.random.fold_in(stream_key, 6), position), (parts,), jnp.float32, least / len(split), top_value / len(split))
        factor_of = factor_of * jnp.repeat(jnp.exp(heights), extent[position] // parts).reshape((-1,) + (1,) * (len(extent) - 1 - position))
    return factor_of


def centred(rng, dims, width, reach, split=(), kind=jnp.bfloat16):
    entries = width * jax.random.normal(rng, dims, jnp.float32)
    if split:
        entries = entries * shard_levels(rng, dims, split, -0.22, 0.18)
    return jnp.clip(entries, -reach, reach).astype(kind)


def setup_inputs(seed: int = 0, part: int = 0) -> dict:
    key_list = jax.random.split(jax.random.key(seed), 9)
    own_keys = jax.random.split(jax.random.fold_in(key_list[8], part), 9)
    return {
        "section_input": centred(own_keys[0], (SECTIONS, TOK, D), 1.0, 6.0, ((0, 16), (2, 16))),
        "stash_pool": centred(own_keys[1], (SECTIONS, SLOTS, TOK, D), 1.0, 6.0, ((0, 16), (3, 16))),
        "reload_slot": set_ends(jax.random.randint(key_list[2], (SECTIONS,), 0, SLOTS), jax.random.fold_in(key_list[2], 1), 0, SLOTS - 1).astype(jnp.int32),
        "cotangent": centred(own_keys[3], (SECTIONS, TOK, D), 1.0, 6.0, ((0, 16), (2, 16))),
        "norm_gain": draw_norm_gain(jax.random.fold_in(key_list[8], 71), part),
        "query_weight": centred(key_list[5], (SECTIONS, D, HEADS * HD), D ** -0.5, 0.09375, ((0, 16), (2, 16))),
        "kv_weight": centred(key_list[6], (SECTIONS, D, 2 * KVH * HD), D ** -0.5, 0.09375, ((0, 16), (1, 16))),
        "out_weight": centred(key_list[7], (SECTIONS, HEADS * HD, D), (HEADS * HD) ** -0.5, 0.09375, ((0, 16), (1, 16))),
    }


norm_eps = 1e-05

def rope_tables(row_total, head_width):
    half_width = head_width // 2
    inverse = 10000.0 ** (-2.0 * jnp.arange(half_width, dtype=jnp.float32) / head_width)
    angles = jnp.arange(row_total, dtype=jnp.float32)[:, None] * inverse[None, :]
    return (jnp.cos(angles)[:, None, :], jnp.sin(angles)[:, None, :])

def rotate(values, cos_table, sin_table):
    half_width = values.shape[-1] // 2
    first_half = values[..., :half_width]
    second_half = values[..., half_width:]
    return jnp.concatenate([first_half * cos_table - second_half * sin_table, second_half * cos_table + first_half * sin_table], axis=-1)

def unrotate(values, cos_table, sin_table):
    half_width = values.shape[-1] // 2
    first_half = values[..., :half_width]
    second_half = values[..., half_width:]
    return jnp.concatenate([first_half * cos_table + second_half * sin_table, second_half * cos_table - first_half * sin_table], axis=-1)

def normalize(token_rows, gain_row):
    rows_wide = token_rows.astype(jnp.float32)
    factor = lax.rsqrt(lax.optimization_barrier(jnp.mean(rows_wide * rows_wide, axis=-1, keepdims=True)) + norm_eps)
    return rows_wide * factor * gain_row

def heads_forward(normed, query_w, kv_w, cos_table, sin_table):
    tokens_here = normed.shape[0]
    kv_all = jnp.dot(normed, kv_w, preferred_element_type=jnp.float32).reshape(tokens_here, 2, KVH, HD)
    key_heads = rotate(kv_all[:, 0], cos_table, sin_table).astype(jnp.bfloat16)
    value_heads = kv_all[:, 1].astype(jnp.bfloat16)
    query_heads = jnp.dot(normed, query_w, preferred_element_type=jnp.float32).reshape(tokens_here, HEADS, HD)
    query_heads = (rotate(query_heads, cos_table, sin_table) * HD ** (-0.5)).astype(jnp.bfloat16)
    grouped = query_heads.reshape(tokens_here, KVH, HEADS // KVH, HD)
    scores = jnp.einsum('tkgd,skd->kgts', grouped.astype(jnp.float32), key_heads.astype(jnp.float32))
    causal = jnp.arange(tokens_here)[:, None] >= jnp.arange(tokens_here)[None, :]
    scores = jnp.where(causal, scores, -1e+30)
    shifted = jnp.exp(scores - lax.optimization_barrier(jnp.max(scores, axis=-1, keepdims=True)))
    softmax_probs = shifted / lax.optimization_barrier(jnp.sum(shifted, axis=-1, keepdims=True))
    prob_weights = softmax_probs.astype(jnp.bfloat16)
    attended = jnp.einsum('kgts,skd->tkgd', prob_weights.astype(jnp.float32), value_heads.astype(jnp.float32))
    attended = attended.astype(jnp.bfloat16).reshape(tokens_here, HEADS * HD)
    return (grouped, key_heads, value_heads, softmax_probs, prob_weights, attended)

def section_forward(token_rows, gain_row, query_w, kv_w, out_w, cos_table, sin_table):
    normed = normalize(token_rows, gain_row).astype(jnp.bfloat16)
    attended = heads_forward(normed, query_w, kv_w, cos_table, sin_table)[5]
    projected = jnp.dot(attended, out_w, preferred_element_type=jnp.float32)
    return (token_rows.astype(jnp.float32) + projected).astype(jnp.bfloat16)

def section_backward(back_rows, cot_rows, gain_row, query_w, kv_w, out_w, cos_table, sin_table):
    tokens_here = back_rows.shape[0]
    normed = normalize(back_rows, gain_row).astype(jnp.bfloat16)
    grouped, key_heads, value_heads, softmax_probs, prob_weights, _ = heads_forward(normed, query_w, kv_w, cos_table, sin_table)
    grad_out = jnp.dot(cot_rows, out_w.T, preferred_element_type=jnp.float32).astype(jnp.bfloat16)
    grad_out = grad_out.reshape(tokens_here, KVH, HEADS // KVH, HD).astype(jnp.float32)
    grad_probs = jnp.einsum('tkgd,skd->kgts', grad_out, value_heads.astype(jnp.float32))
    row_delta = lax.optimization_barrier(jnp.sum(softmax_probs * grad_probs, axis=-1, keepdims=True))
    grad_scores = (softmax_probs * (grad_probs - row_delta)).astype(jnp.bfloat16).astype(jnp.float32)
    grad_query = jnp.einsum('kgts,skd->tkgd', grad_scores, key_heads.astype(jnp.float32)).reshape(tokens_here, HEADS, HD)
    grad_query = (unrotate(grad_query, cos_table, sin_table) * HD ** (-0.5)).astype(jnp.bfloat16).reshape(tokens_here, HEADS * HD)
    grad_key = jnp.einsum('kgts,tkgd->skd', grad_scores, grouped.astype(jnp.float32))
    grad_key = unrotate(grad_key, cos_table, sin_table)
    grad_value = jnp.einsum('kgts,tkgd->skd', prob_weights.astype(jnp.float32), grad_out)
    grad_kv = jnp.stack([grad_key, grad_value], axis=1).reshape(tokens_here, 2 * KVH * HD).astype(jnp.bfloat16)
    grad_normed = jnp.dot(grad_query, query_w.T, preferred_element_type=jnp.float32) + jnp.dot(grad_kv, kv_w.T, preferred_element_type=jnp.float32)
    rows_wide = back_rows.astype(jnp.float32)
    factor = lax.rsqrt(lax.optimization_barrier(jnp.mean(rows_wide * rows_wide, axis=-1, keepdims=True)) + norm_eps)
    scaled = grad_normed * gain_row
    grad_rows = factor * scaled - rows_wide * factor * factor * factor * lax.optimization_barrier(jnp.mean(scaled * rows_wide, axis=-1, keepdims=True))
    return (cot_rows.astype(jnp.float32) + grad_rows).astype(jnp.bfloat16)

def reference(section_input, stash_pool, reload_slot, cotangent, norm_gain, query_weight, kv_weight, out_weight):
    cos_table, sin_table = rope_tables(TOK, HD)
    section_ids = jnp.arange(SECTIONS, dtype=jnp.int32)
    is_early = (section_ids < SECTIONS // 2)[:, None, None]
    picked = stash_pool[section_ids, reload_slot.astype(jnp.int32)]
    sending = jnp.where(is_early, section_input, picked)
    received = sending[::-1]
    back_input = jnp.where(is_early, received, section_input)

    def per_section(pieces):
        token_rows, back_rows, cot_rows, gain_row, query_w, kv_w, out_w = pieces
        layer_out = section_forward(token_rows, gain_row, query_w, kv_w, out_w, cos_table, sin_table)
        grad_local = section_backward(back_rows, cot_rows, gain_row, query_w, kv_w, out_w, cos_table, sin_table)
        return (layer_out, grad_local)
    layer_outputs, layer_grads = lax.map(per_section, (section_input, back_input, cotangent, norm_gain, query_weight, kv_weight, out_weight))
    zero_block = jnp.zeros_like(layer_outputs[:1])
    next_input = jnp.concatenate([zero_block, layer_outputs[:-1]], axis=0)
    input_grad = jnp.concatenate([layer_grads[1:], zero_block], axis=0)
    return (next_input, received, input_grad)
```

```python
import functools

import jax
import jax.numpy as jnp
import numpy as np
from jax import lax
from jax.experimental import pallas as pl
from jax.experimental.pallas import tpu as pltpu
from jax.sharding import PartitionSpec as P

HEADS = 32
KVH = 4
HD = 128
TOK = 128
WIDTH = 4096
COLS = 256
SIDE = 4
norm_eps = 1e-05
MIB = 1024 * 1024

ALONG_Y = [[x * SIDE + y for y in range(SIDE)] for x in range(SIDE)]
ALONG_X = [[x * SIDE + y for x in range(SIDE)] for y in range(SIDE)]

NN = (((1,), (0,)), ((), ()))
NT = (((1,), (1,)), ((), ()))
TN = (((0,), (0,)), ((), ()))


def rope_angles():
    inverse = 10000.0 ** (-2.0 * np.arange(HD // 2, dtype=np.float64) / HD)
    angles = np.arange(TOK, dtype=np.float64)[:, None] * inverse[None, :]
    return np.cos(angles).astype(np.float32), np.sin(angles).astype(np.float32)


def matmul(left, right, dims):
    return lax.dot_general(left, right, dims, preferred_element_type=jnp.float32)


def exchange(blocks, groups):
    return lax.all_to_all(blocks, "tensor", 0, 0, axis_index_groups=groups)


def call(kernel, outs, *operands, vmem=32, flops=0):
    nbytes = sum(int(np.prod(a.shape)) * a.dtype.itemsize for a in (*operands, *outs))
    return pl.pallas_call(
        kernel,
        out_shape=outs,
        compiler_params=pltpu.CompilerParams(vmem_limit_bytes=vmem * MIB),
        cost_estimate=pl.CostEstimate(flops=flops, bytes_accessed=nbytes, transcendentals=0),
    )(*operands)


def shape(dims, dtype=jnp.bfloat16):
    return jax.ShapeDtypeStruct(dims, dtype)


def pack_kv_weight(w_ref, out_ref):
    for x in range(SIDE):
        keys = w_ref[:, x * HD : (x + 1) * HD].T
        values = w_ref[:, (KVH + x) * HD : (KVH + x + 1) * HD].T
        for y in range(SIDE):
            out_ref[x * SIDE + y, 0:16] = keys[16 * y : 16 * y + 16]
            out_ref[x * SIDE + y, 16:32] = keys[64 + 16 * y : 80 + 16 * y]
            out_ref[x * SIDE + y, 32:64] = values[32 * y : 32 * y + 32]


def norm_and_kv(rows_ref, kvw_ref, cos_ref, sin_ref, normed_ref, kv_ref, raw_ref, factor_ref):
    total = jnp.zeros((2 * TOK, 1), jnp.float32)
    for x in range(SIDE):
        for y in range(SIDE):
            block = rows_ref[x, y * 384 : y * 384 + 256].astype(jnp.float32)
            total = total + jnp.sum(block * block, axis=1, keepdims=True)
    factor = lax.rsqrt(total / WIDTH + norm_eps)
    factor_ref[...] = jnp.broadcast_to(factor[TOK:], (TOK, HD))
    kv = jnp.zeros((64, 2 * TOK), jnp.float32)
    for x in range(SIDE):
        gains = rows_ref[x, 1536:1552].astype(jnp.float32)
        for y in range(SIDE):
            gain = gains[3 * y : 3 * y + 1] + gains[3 * y + 1 : 3 * y + 2] + gains[3 * y + 2 : 3 * y + 3]
            block = rows_ref[x, y * 384 : y * 384 + 256].astype(jnp.float32)
            normed = (block * factor * gain).astype(jnp.bfloat16)
            normed_ref[x * SIDE + y] = normed
            kv = kv + matmul(kvw_ref[x * SIDE + y], normed, NT)
    raw_ref[...] = kv[:, TOK:]
    first, second = kv[0:16], kv[16:32]
    cos, sin = cos_ref[...], sin_ref[...]
    out = jnp.concatenate([first * cos - second * sin, second * cos + first * sin, kv[32:64]], axis=0)
    out = out.astype(jnp.bfloat16)
    for y in range(SIDE):
        kv_ref[y] = out


def attention(
    rows_ref, normed_ref, kv_ref, qw_ref, ow_ref, cos_ref, sin_ref, cost_ref, sint_ref,
    attended_ref, grad_query_ref, grad_kv_ref, mixed_ref,
):
    query = jnp.zeros((2 * TOK, COLS), jnp.float32)
    grad_out = jnp.zeros((TOK, COLS), jnp.float32)
    for x in range(SIDE):
        for y in range(SIDE):
            t = x * SIDE + y
            query = query + matmul(normed_ref[t], qw_ref[t * COLS : (t + 1) * COLS], NN)
            cot = rows_ref[x, y * 384 + 256 : y * 384 + 384]
            grad_out = grad_out + matmul(cot, ow_ref[:, t * COLS : (t + 1) * COLS], NT)
    grad_out = grad_out.astype(jnp.bfloat16)
    kv = [kv_ref[y] for y in range(SIDE)]
    cos, sin = cos_ref[...], sin_ref[...]
    scale = HD ** (-0.5)
    causal = lax.broadcasted_iota(jnp.int32, (TOK, TOK), 0) >= lax.broadcasted_iota(
        jnp.int32, (TOK, TOK), 1
    )

    def softmax(scores):
        scores = jnp.where(causal, scores, -1e30)
        shifted = jnp.exp(scores - jnp.max(scores, axis=-1, keepdims=True))
        return shifted / jnp.sum(shifted, axis=-1, keepdims=True)

    def keys_values(start):
        part = [k[:, start : start + TOK] for k in kv]
        keys = jnp.concatenate([p[0:16] for p in part] + [p[16:32] for p in part], axis=0)
        return keys, jnp.concatenate([p[32:64] for p in part], axis=0)

    def heads(start, h):
        raw = query[start : start + TOK, h * HD : (h + 1) * HD]
        turned = raw * cos + pltpu.roll(raw, HD // 2, 1) * sin
        return raw, (turned * scale).astype(jnp.bfloat16)

    keys, values = keys_values(0)
    for h in range(2):
        _, query_head = heads(0, h)
        weights = softmax(matmul(query_head, keys, NN)).astype(jnp.bfloat16)
        attended_ref[:, h * HD : (h + 1) * HD] = matmul(weights, values, NT).astype(jnp.bfloat16)

    keys, values = keys_values(TOK)
    grad_key = jnp.zeros((HD, TOK), jnp.float32)
    grad_value = jnp.zeros((HD, TOK), jnp.float32)
    mixed = jnp.zeros((TOK, HD), jnp.float32)
    for h in range(2):
        raw, query_head = heads(TOK, h)
        probs = softmax(matmul(query_head, keys, NN))
        grad_head = grad_out[:, h * HD : (h + 1) * HD]
        grad_probs = matmul(grad_head, values, NN)
        delta = jnp.sum(probs * grad_probs, axis=-1, keepdims=True)
        grad_scores = (probs * (grad_probs - delta)).astype(jnp.bfloat16)
        turned = matmul(grad_scores, keys, NT)
        grad_query = (turned * cos - pltpu.roll(turned, HD // 2, 1) * sin) * scale
        grad_query = grad_query.astype(jnp.bfloat16)
        grad_query_ref[:, h * HD : (h + 1) * HD] = grad_query
        mixed = mixed + grad_query.astype(jnp.float32) * raw
        grad_key = grad_key + matmul(query_head, grad_scores, TN)
        grad_value = grad_value + matmul(grad_head, probs.astype(jnp.bfloat16), TN)
    cost, sint = cost_ref[...], sint_ref[...]
    first, second = grad_key[:64], grad_key[64:]
    key_first = first * cost + second * sint
    key_second = second * cost - first * sint
    for y in range(SIDE):
        grad_kv_ref[y, 0:16] = key_first[16 * y : 16 * y + 16]
        grad_kv_ref[y, 16:32] = key_second[16 * y : 16 * y + 16]
        grad_kv_ref[y, 32:64] = grad_value[32 * y : 32 * y + 32]
    mixed_ref[...] = jnp.broadcast_to(jnp.sum(mixed.T, axis=0, keepdims=True), (8, TOK))


def split_rows(total):
    high = total.astype(jnp.bfloat16)
    low = (total - high.astype(jnp.float32)).astype(jnp.bfloat16)
    row = lax.broadcasted_iota(jnp.int32, (16, TOK), 0)
    both = jnp.where(row == 0, high.astype(jnp.float32), low.astype(jnp.float32))
    both = jnp.where(row < 2, both, 0.0)
    return jnp.concatenate([both, jnp.zeros((16, COLS - TOK), jnp.float32)], axis=1).astype(jnp.bfloat16)


def project(attended_ref, grad_query_ref, grad_kv_ref, raw_ref, mixed_ref, qw_ref, ow_ref, kvw_ref, out_ref):
    attended = attended_ref[...]
    grad_query = grad_query_ref[...]
    grad_kv = grad_kv_ref[0] + grad_kv_ref[1] + grad_kv_ref[2] + grad_kv_ref[3]
    grad_kv = grad_kv.astype(jnp.bfloat16)
    mixed = mixed_ref[0:1] + jnp.sum(grad_kv.astype(jnp.float32) * raw_ref[...], axis=0, keepdims=True)
    rows = split_rows(mixed)
    for x in range(SIDE):
        for y in range(SIDE):
            t = x * SIDE + y
            term = matmul(attended, ow_ref[:, t * COLS : (t + 1) * COLS], NN)
            out_ref[x, y * 256 : y * 256 + TOK] = term.astype(jnp.bfloat16)
            term = matmul(grad_query, qw_ref[t * COLS : (t + 1) * COLS], NT)
            term = term + matmul(grad_kv, kvw_ref[t], TN)
            out_ref[x, y * 256 + TOK : y * 256 + 256] = term.astype(jnp.bfloat16)
        out_ref[x, 1024:1040] = rows


def sum_x(parts_ref, out_ref):
    rows = parts_ref[0, 1024:1040].astype(jnp.float32)
    for x in range(1, SIDE):
        rows = rows + parts_ref[x, 1024:1040].astype(jnp.float32)
    mixed = split_rows(rows[0:1, :TOK] + rows[1:2, :TOK])
    for y in range(SIDE):
        total = parts_ref[0, y * 256 : y * 256 + 256].astype(jnp.float32)
        for x in range(1, SIDE):
            total = total + parts_ref[x, y * 256 : y * 256 + 256].astype(jnp.float32)
        out_ref[y, 0:256] = total.astype(jnp.bfloat16)
        out_ref[y, 256:272] = mixed


def finish(parts_ref, rows_ref, back_ref, cot_ref, gain_ref, factor_ref, out_ref, grad_ref):
    total = parts_ref[0].astype(jnp.float32)
    for y in range(1, SIDE):
        total = total + parts_ref[y].astype(jnp.float32)
    out_ref[...] = (rows_ref[...].astype(jnp.float32) + total[0:TOK]).astype(jnp.bfloat16)
    mixed = jnp.broadcast_to(total[256:257, :TOK] + total[257:258, :TOK], (TOK, TOK)).T[:, 0:1]
    factor = factor_ref[:, 0:1]
    scaled = total[TOK : 2 * TOK] * gain_ref[...]
    grad_rows = factor * scaled - back_ref[...].astype(jnp.float32) * (factor * factor * mixed / WIDTH)
    grad_ref[...] = (cot_ref[...].astype(jnp.float32) + grad_rows).astype(jnp.bfloat16)


def per_device(
    section_input,
    stash_pool,
    reload_slot,
    cotangent,
    norm_gain,
    query_weight,
    kv_weight,
    out_weight,
):
    token_rows = section_input[0]
    cot_rows = cotangent[0]
    query_w = query_weight[0]
    kv_w = kv_weight[0]
    out_w = out_weight[0]
    section_count = lax.axis_size("section")
    section_pos = lax.axis_index("section")
    is_early = section_pos < section_count // 2
    y_pos = lax.axis_index("tensor") % SIDE

    picked = lax.dynamic_index_in_dim(stash_pool[0], reload_slot[0], 0, keepdims=False)
    sending = jnp.where(is_early, token_rows, picked)
    mirrored = [(s, section_count - 1 - s) for s in range(section_count)]
    received = lax.ppermute(sending, "section", mirrored)
    back_rows = jnp.where(is_early, received, token_rows)

    packed = call(pack_kv_weight, (shape((16, 64, COLS)),), kv_w)[0]
    kv_rows = lax.all_to_all(packed, "tensor", 0, 0)

    gain_row = norm_gain
    high = lax.reduce_precision(gain_row, 8, 7)
    middle = lax.reduce_precision(gain_row - high, 8, 7)
    low = gain_row - high - middle
    gains = jnp.concatenate([high, middle, low, jnp.zeros((13, COLS), jnp.float32)], axis=0)
    own = jnp.concatenate([token_rows, back_rows, cot_rows, gains.astype(jnp.bfloat16)], axis=0)
    column = exchange(jnp.broadcast_to(own[None], (SIDE,) + own.shape), ALONG_Y)
    gains = jnp.concatenate(
        [column[:, 384:387].reshape(12, COLS), jnp.zeros((4, COLS), jnp.bfloat16)], axis=0
    )
    column = jnp.concatenate([column[:, :384].reshape(1536, COLS), gains], axis=0)
    rows = exchange(jnp.broadcast_to(column[None], (SIDE,) + column.shape), ALONG_X)

    cos, sin = rope_angles()
    cos_cols, sin_cols = jnp.asarray(cos.T.copy()), jnp.asarray(sin.T.copy())
    wide = np.concatenate([cos, cos], axis=1), np.concatenate([-sin, sin], axis=1)
    cos_wide, sin_wide = jnp.asarray(wide[0]), jnp.asarray(wide[1])
    cos_own = jnp.tile(lax.dynamic_slice_in_dim(cos_cols, 16 * y_pos, 16, 0), (1, 2))
    sin_own = jnp.tile(lax.dynamic_slice_in_dim(sin_cols, 16 * y_pos, 16, 0), (1, 2))
    normed, kv_own, kv_raw, factor = call(
        norm_and_kv,
        (
            shape((16, 2 * TOK, COLS)),
            shape((SIDE, 64, 2 * TOK)),
            shape((64, TOK), jnp.float32),
            shape((TOK, HD), jnp.float32),
        ),
        rows, kv_rows, cos_own, sin_own,
        flops=2 * 64 * 256 * 4096,
    )
    kv_all = exchange(kv_own, ALONG_Y)
    attended, grad_query, grad_kv, mixed = call(
        attention,
        (
            shape((TOK, COLS)),
            shape((TOK, COLS)),
            shape((SIDE, 64, TOK), jnp.float32),
            shape((8, TOK), jnp.float32),
        ),
        rows, normed, kv_all, query_w, out_w, cos_wide, sin_wide, cos_cols, sin_cols,
        flops=2 * 384 * 256 * 4096,
    )
    grad_kv = exchange(grad_kv, ALONG_Y)
    terms = call(
        project,
        (shape((SIDE, 1040, COLS)),),
        attended, grad_query, grad_kv, kv_raw, mixed, query_w, out_w, kv_rows,
        flops=2 * 256 * 256 * 4096,
    )[0]
    terms = exchange(terms, ALONG_X)
    terms = call(sum_x, (shape((SIDE, 272, COLS)),), terms)[0]
    terms = exchange(terms, ALONG_Y)
    layer_out, grad_local = call(
        finish,
        (shape((TOK, COLS)), shape((TOK, COLS))),
        terms, token_rows, back_rows, cot_rows, gain_row, factor,
    )
    next_input = lax.ppermute(layer_out, "section", [(s, s + 1) for s in range(section_count - 1)])
    input_grad = lax.ppermute(grad_local, "section", [(s + 1, s) for s in range(section_count - 1)])
    return (next_input[None], received[None], input_grad[None])


def solution(mesh):
    return jax.shard_map(
        per_device,
        mesh=mesh,
        in_specs=(
            P("section", "dp", "tensor"),
            P("section", None, "dp", "tensor"),
            P("section"),
            P("section", "dp", "tensor"),
            P("section", "tensor"),
            P("section", None, "tensor"),
            P("section", "tensor", None),
            P("section", "tensor", None),
        ),
        out_specs=(
            P("section", "dp", "tensor"),
            P("section", "dp", "tensor"),
            P("section", "dp", "tensor"),
        ),
        check_vma=False,
    )
```

```python
import functools

import jax
import jax.numpy as jnp
import numpy as np
from jax import lax
from jax.experimental import pallas as pl
from jax.experimental.pallas import tpu as pltpu
from jax.sharding import PartitionSpec as P

HEADS = 32
KVH = 4
HD = 128
TOK = 128
WIDTH = 4096
COLS = 256
SIDE = 4
norm_eps = 1e-05
MIB = 1024 * 1024

ALONG_Y = [[x * SIDE + y for y in range(SIDE)] for x in range(SIDE)]

NN = (((1,), (0,)), ((), ()))
NT = (((1,), (1,)), ((), ()))
TN = (((0,), (0,)), ((), ()))


def rope_angles():
    inverse = 10000.0 ** (-2.0 * np.arange(HD // 2, dtype=np.float64) / HD)
    angles = np.arange(TOK, dtype=np.float64)[:, None] * inverse[None, :]
    return np.cos(angles).astype(np.float32), np.sin(angles).astype(np.float32)


def matmul(left, right, dims):
    return lax.dot_general(left, right, dims, preferred_element_type=jnp.float32)


def exchange(blocks, groups):
    return lax.all_to_all(blocks, "tensor", 0, 0, axis_index_groups=groups)


def around_x(t, k):
    return (t // SIDE + k) % SIDE * SIDE + t % SIDE


def from_ahead(block, k):
    return lax.ppermute(block, "tensor", [(around_x(t, k), t) for t in range(16)])


def to_ahead(block, k):
    return lax.ppermute(block, "tensor", [(t, around_x(t, k)) for t in range(16)])


def call(kernel, outs, *operands, vmem=32, flops=0):
    nbytes = sum(int(np.prod(a.shape)) * a.dtype.itemsize for a in (*operands, *outs))
    specs = [
        pl.BlockSpec(memory_space=pltpu.SMEM if a.shape == (1,) else pltpu.VMEM) for a in operands
    ]
    return pl.pallas_call(
        kernel,
        out_shape=outs,
        in_specs=specs,
        compiler_params=pltpu.CompilerParams(vmem_limit_bytes=vmem * MIB),
        cost_estimate=pl.CostEstimate(flops=flops, bytes_accessed=nbytes, transcendentals=0),
    )(*operands)


def shape(dims, dtype=jnp.bfloat16):
    return jax.ShapeDtypeStruct(dims, dtype)


def pack_kv_weight(w_ref, out_ref):
    for x in range(SIDE):
        keys = w_ref[:, x * HD : (x + 1) * HD].T
        values = w_ref[:, (KVH + x) * HD : (KVH + x + 1) * HD].T
        for y in range(SIDE):
            out_ref[x * SIDE + y, 0:16] = keys[16 * y : 16 * y + 16]
            out_ref[x * SIDE + y, 16:32] = keys[64 + 16 * y : 80 + 16 * y]
            out_ref[x * SIDE + y, 32:64] = values[32 * y : 32 * y + 32]


def source_block(x_ref, k):
    return lax.rem(x_ref[0] + k, SIDE)


def norm_and_kv(
    x_ref, f0, f1, f2, f3, b0, b1, b2, b3, kvw_ref, cos_ref, sin_ref, normed_ref, kv_ref, raw_ref, factor_ref
):
    ahead, back = (f0, f1, f2, f3), (b0, b1, b2, b3)
    total = jnp.zeros((TOK, COLS), jnp.float32)
    back_total = jnp.zeros((TOK, COLS), jnp.float32)
    for k in range(SIDE):
        for y in range(SIDE):
            block = ahead[k][y * 256 : y * 256 + TOK].astype(jnp.float32)
            total = total + block * block
            block = back[k][y * TOK : (y + 1) * TOK].astype(jnp.float32)
            back_total = back_total + block * block
    factor = lax.rsqrt(jnp.sum(total, axis=1, keepdims=True) / WIDTH + norm_eps)
    back_factor = lax.rsqrt(jnp.sum(back_total, axis=1, keepdims=True) / WIDTH + norm_eps)
    factor_ref[...] = jnp.broadcast_to(back_factor, (TOK, HD))
    kv = jnp.zeros((64, 2 * TOK), jnp.float32)
    for k in range(SIDE):
        gains = ahead[k][1024:1040].astype(jnp.float32)
        for y in range(SIDE):
            t = source_block(x_ref, k) * SIDE + y
            gain = gains[3 * y : 3 * y + 1] + gains[3 * y + 1 : 3 * y + 2] + gains[3 * y + 2 : 3 * y + 3]
            block = ahead[k][y * 256 : y * 256 + TOK].astype(jnp.float32)
            normed = (block * factor * gain).astype(jnp.bfloat16)
            block = back[k][y * TOK : (y + 1) * TOK].astype(jnp.float32)
            back_normed = (block * back_factor * gain).astype(jnp.bfloat16)
            normed = jnp.concatenate([normed, back_normed], axis=0)
            normed_ref[k * SIDE + y] = normed
            kv = kv + matmul(kvw_ref[t], normed, NT)
    raw_ref[...] = kv[:, TOK:]
    first, second = kv[0:16], kv[16:32]
    cos, sin = cos_ref[...], sin_ref[...]
    out = jnp.concatenate([first * cos - second * sin, second * cos + first * sin, kv[32:64]], axis=0)
    out = out.astype(jnp.bfloat16)
    for y in range(SIDE):
        kv_ref[y] = out


def weight_rows(t):
    return pl.ds(pl.multiple_of(t * COLS, COLS), COLS)


def queries(x_ref, normed_ref, f0, f1, f2, f3, qw_ref, ow_ref, query_ref, grad_out_ref):
    ahead = (f0, f1, f2, f3)
    query = jnp.zeros((2 * TOK, COLS), jnp.float32)
    grad_out = jnp.zeros((TOK, COLS), jnp.float32)
    for k in range(SIDE):
        for y in range(SIDE):
            block = weight_rows(source_block(x_ref, k) * SIDE + y)
            query = query + matmul(normed_ref[k * SIDE + y], qw_ref[block, :], NN)
            cot = ahead[k][y * 256 + TOK : y * 256 + 256]
            grad_out = grad_out + matmul(cot, ow_ref[:, block], NT)
    query_ref[...] = query
    grad_out_ref[...] = grad_out.astype(jnp.bfloat16)


def attention(
    query_ref, grad_out_ref, kv_ref, cos_ref, sin_ref, cost_ref, sint_ref,
    attended_ref, grad_query_ref, grad_kv_ref, mixed_ref,
):
    query = query_ref[...]
    grad_out = grad_out_ref[...]
    kv = [kv_ref[y] for y in range(SIDE)]
    cos, sin = cos_ref[...], sin_ref[...]
    scale = HD ** (-0.5)
    causal = lax.broadcasted_iota(jnp.int32, (TOK, TOK), 0) >= lax.broadcasted_iota(
        jnp.int32, (TOK, TOK), 1
    )

    def softmax(scores):
        scores = jnp.where(causal, scores, -1e30)
        shifted = jnp.exp(scores - jnp.max(scores, axis=-1, keepdims=True))
        return shifted / jnp.sum(shifted, axis=-1, keepdims=True)

    def keys_values(start):
        part = [k[:, start : start + TOK] for k in kv]
        keys = jnp.concatenate([p[0:16] for p in part] + [p[16:32] for p in part], axis=0)
        return keys, jnp.concatenate([p[32:64] for p in part], axis=0)

    def heads(start, h):
        raw = query[start : start + TOK, h * HD : (h + 1) * HD]
        turned = raw * cos + pltpu.roll(raw, HD // 2, 1) * sin
        return raw, (turned * scale).astype(jnp.bfloat16)

    keys, values = keys_values(0)
    for h in range(2):
        _, query_head = heads(0, h)
        weights = softmax(matmul(query_head, keys, NN)).astype(jnp.bfloat16)
        attended_ref[:, h * HD : (h + 1) * HD] = matmul(weights, values, NT).astype(jnp.bfloat16)

    keys, values = keys_values(TOK)
    grad_key = jnp.zeros((HD, TOK), jnp.float32)
    grad_value = jnp.zeros((HD, TOK), jnp.float32)
    mixed = jnp.zeros((TOK, HD), jnp.float32)
    for h in range(2):
        raw, query_head = heads(TOK, h)
        probs = softmax(matmul(query_head, keys, NN))
        grad_head = grad_out[:, h * HD : (h + 1) * HD]
        grad_probs = matmul(grad_head, values, NN)
        delta = jnp.sum(probs * grad_probs, axis=-1, keepdims=True)
        grad_scores = (probs * (grad_probs - delta)).astype(jnp.bfloat16)
        turned = matmul(grad_scores, keys, NT)
        grad_query = (turned * cos - pltpu.roll(turned, HD // 2, 1) * sin) * scale
        grad_query = grad_query.astype(jnp.bfloat16)
        grad_query_ref[:, h * HD : (h + 1) * HD] = grad_query
        mixed = mixed + grad_query.astype(jnp.float32) * raw
        grad_key = grad_key + matmul(query_head, grad_scores, TN)
        grad_value = grad_value + matmul(grad_head, probs.astype(jnp.bfloat16), TN)
    cost, sint = cost_ref[...], sint_ref[...]
    first, second = grad_key[:64], grad_key[64:]
    key_first = first * cost + second * sint
    key_second = second * cost - first * sint
    for y in range(SIDE):
        grad_kv_ref[y, 0:16] = key_first[16 * y : 16 * y + 16]
        grad_kv_ref[y, 16:32] = key_second[16 * y : 16 * y + 16]
        grad_kv_ref[y, 32:64] = grad_value[32 * y : 32 * y + 32]
    mixed_ref[...] = jnp.broadcast_to(jnp.sum(mixed.T, axis=0, keepdims=True), (8, TOK))


def split_rows(total):
    high = total.astype(jnp.bfloat16)
    low = (total - high.astype(jnp.float32)).astype(jnp.bfloat16)
    row = lax.broadcasted_iota(jnp.int32, (16, TOK), 0)
    both = jnp.where(row == 0, high.astype(jnp.float32), low.astype(jnp.float32))
    both = jnp.where(row < 2, both, 0.0)
    return jnp.concatenate([both, jnp.zeros((16, COLS - TOK), jnp.float32)], axis=1).astype(jnp.bfloat16)


def project_out(x_ref, attended_ref, ow_ref, o0, o1, o2, o3):
    attended = attended_ref[...]
    for k, out_ref in enumerate((o0, o1, o2, o3)):
        for y in range(SIDE):
            block = weight_rows(source_block(x_ref, k) * SIDE + y)
            term = matmul(attended, ow_ref[:, block], NN)
            out_ref[y * TOK : (y + 1) * TOK] = term.astype(jnp.bfloat16)


def project_grad(
    x_ref, grad_query_ref, grad_kv_ref, raw_ref, mixed_ref, qw_ref, kvw_ref, o0, o1, o2, o3
):
    grad_query = grad_query_ref[...]
    grad_kv = grad_kv_ref[0] + grad_kv_ref[1] + grad_kv_ref[2] + grad_kv_ref[3]
    grad_kv = grad_kv.astype(jnp.bfloat16)
    mixed = mixed_ref[0:1] + jnp.sum(grad_kv.astype(jnp.float32) * raw_ref[...], axis=0, keepdims=True)
    rows = split_rows(mixed)
    for k, out_ref in enumerate((o0, o1, o2, o3)):
        for y in range(SIDE):
            t = source_block(x_ref, k) * SIDE + y
            term = matmul(grad_query, qw_ref[weight_rows(t), :], NT)
            term = term + matmul(grad_kv, kvw_ref[t], TN)
            out_ref[y * TOK : (y + 1) * TOK] = term.astype(jnp.bfloat16)
        out_ref[512:528] = rows


def sum_out(p0, p1, p2, p3, out_ref):
    for y in range(SIDE):
        total = jnp.zeros((TOK, COLS), jnp.float32)
        for part in (p0, p1, p2, p3):
            total = total + part[y * TOK : (y + 1) * TOK].astype(jnp.float32)
        out_ref[y, 0:TOK] = total.astype(jnp.bfloat16)


def sum_grad(p0, p1, p2, p3, out_ref):
    sum_out(p0, p1, p2, p3, out_ref)
    rows = jnp.zeros((16, COLS), jnp.float32)
    for part in (p0, p1, p2, p3):
        rows = rows + part[512:528].astype(jnp.float32)
    mixed = split_rows(rows[0:1, :TOK] + rows[1:2, :TOK])
    for y in range(SIDE):
        out_ref[y, TOK : TOK + 16] = mixed


def finish_out(parts_ref, rows_ref, out_ref):
    total = rows_ref[...].astype(jnp.float32)
    for y in range(SIDE):
        total = total + parts_ref[y].astype(jnp.float32)
    out_ref[...] = total.astype(jnp.bfloat16)


def finish_grad(parts_ref, back_ref, cot_ref, gain_ref, factor_ref, grad_ref):
    total = parts_ref[0].astype(jnp.float32)
    for y in range(1, SIDE):
        total = total + parts_ref[y].astype(jnp.float32)
    mixed = jnp.broadcast_to(total[TOK : TOK + 1, :TOK] + total[TOK + 1 : TOK + 2, :TOK], (TOK, TOK))
    mixed = mixed.T[:, 0:1]
    factor = factor_ref[:, 0:1]
    scaled = total[0:TOK] * gain_ref[...]
    grad_rows = factor * scaled - back_ref[...].astype(jnp.float32) * (factor * factor * mixed / WIDTH)
    grad_ref[...] = (cot_ref[...].astype(jnp.float32) + grad_rows).astype(jnp.bfloat16)


def per_device(
    section_input,
    stash_pool,
    reload_slot,
    cotangent,
    norm_gain,
    query_weight,
    kv_weight,
    out_weight,
):
    token_rows = section_input[0]
    cot_rows = cotangent[0]
    query_w = query_weight[0]
    kv_w = kv_weight[0]
    out_w = out_weight[0]
    section_count = lax.axis_size("section")
    section_pos = lax.axis_index("section")
    is_early = section_pos < section_count // 2
    y_pos = lax.axis_index("tensor") % SIDE

    picked = lax.dynamic_index_in_dim(stash_pool[0], reload_slot[0], 0, keepdims=False)
    sending = jnp.where(is_early, token_rows, picked)
    mirrored = [(s, section_count - 1 - s) for s in range(section_count)]
    received = lax.ppermute(sending, "section", mirrored)
    back_rows = jnp.where(is_early, received, token_rows)

    x_pos = (lax.axis_index("tensor") // SIDE).astype(jnp.int32).reshape(1)
    gain_row = norm_gain
    high = lax.reduce_precision(gain_row, 8, 7)
    middle = lax.reduce_precision(gain_row - high, 8, 7)
    low = gain_row - high - middle
    gains = jnp.concatenate([high, middle, low, jnp.zeros((13, COLS), jnp.float32)], axis=0)
    own = jnp.concatenate([token_rows, cot_rows, gains.astype(jnp.bfloat16)], axis=0)
    column = exchange(jnp.broadcast_to(own[None], (SIDE,) + own.shape), ALONG_Y)
    back_rows, _ = lax.optimization_barrier((back_rows, column))
    back_column = exchange(jnp.broadcast_to(back_rows[None], (SIDE,) + back_rows.shape), ALONG_Y)
    gains = jnp.concatenate(
        [column[:, 256:259].reshape(12, COLS), jnp.zeros((4, COLS), jnp.bfloat16)], axis=0
    )
    column = jnp.concatenate([column[:, :256].reshape(1024, COLS), gains], axis=0)
    ahead = [column] + [from_ahead(column, k) for k in range(1, SIDE)]
    kv_w, _ = lax.optimization_barrier((kv_w, back_column))
    back_column = back_column.reshape(4 * TOK, COLS)
    back = [back_column] + [from_ahead(back_column, k) for k in range(1, SIDE)]

    packed = call(pack_kv_weight, (shape((16, 64, COLS)),), kv_w)[0]
    kv_rows = lax.all_to_all(packed, "tensor", 0, 0)

    cos, sin = rope_angles()
    cos_cols, sin_cols = jnp.asarray(cos.T.copy()), jnp.asarray(sin.T.copy())
    wide = np.concatenate([cos, cos], axis=1), np.concatenate([-sin, sin], axis=1)
    cos_wide, sin_wide = jnp.asarray(wide[0]), jnp.asarray(wide[1])
    cos_own = jnp.tile(lax.dynamic_slice_in_dim(cos_cols, 16 * y_pos, 16, 0), (1, 2))
    sin_own = jnp.tile(lax.dynamic_slice_in_dim(sin_cols, 16 * y_pos, 16, 0), (1, 2))
    normed, kv_own, kv_raw, factor = call(
        norm_and_kv,
        (
            shape((16, 2 * TOK, COLS)),
            shape((SIDE, 64, 2 * TOK)),
            shape((64, TOK), jnp.float32),
            shape((TOK, HD), jnp.float32),
        ),
        x_pos, *ahead, *back, kv_rows, cos_own, sin_own,
        flops=2 * 64 * 256 * 4096,
    )
    kv_all = exchange(kv_own, ALONG_Y)
    query, grad_out = call(
        queries,
        (shape((2 * TOK, COLS), jnp.float32), shape((TOK, COLS))),
        x_pos, normed, *ahead, query_w, out_w,
        flops=2 * 384 * 256 * 4096,
    )
    attended, grad_query, grad_kv, mixed = call(
        attention,
        (
            shape((TOK, COLS)),
            shape((TOK, COLS)),
            shape((SIDE, 64, TOK), jnp.float32),
            shape((8, TOK), jnp.float32),
        ),
        query, grad_out, kv_all, cos_wide, sin_wide, cos_cols, sin_cols,
    )
    grad_kv = exchange(grad_kv, ALONG_Y)
    out_terms = call(
        project_out,
        (shape((4 * TOK, COLS)),) * SIDE,
        x_pos, attended, out_w,
        flops=2 * 128 * 256 * 4096,
    )
    out_terms = [out_terms[0]] + [to_ahead(out_terms[k], k) for k in range(1, SIDE)]
    out_terms = call(sum_out, (shape((SIDE, TOK, COLS)),), *out_terms)[0]
    out_terms, _ = lax.optimization_barrier((out_terms, grad_kv))
    out_terms = exchange(out_terms, ALONG_Y)
    layer_out = call(finish_out, (shape((TOK, COLS)),), out_terms, token_rows)[0]
    next_input = lax.ppermute(layer_out, "section", [(s, s + 1) for s in range(section_count - 1)])

    terms = call(
        project_grad,
        (shape((4 * TOK + 16, COLS)),) * SIDE,
        x_pos, grad_query, grad_kv, kv_raw, mixed, query_w, kv_rows,
        flops=2 * 128 * 256 * 4096,
    )
    terms = [terms[0]] + [to_ahead(terms[k], k) for k in range(1, SIDE)]
    terms = call(sum_grad, (shape((SIDE, TOK + 16, COLS)),), *terms)[0]
    terms, _ = lax.optimization_barrier((terms, out_terms))
    terms = exchange(terms, ALONG_Y)
    grad_local = call(
        finish_grad,
        (shape((TOK, COLS)),),
        terms, back_rows, cot_rows, gain_row, factor,
    )[0]
    input_grad = lax.ppermute(grad_local, "section", [(s + 1, s) for s in range(section_count - 1)])
    return (next_input[None], received[None], input_grad[None])


def solution(mesh):
    return jax.shard_map(
        per_device,
        mesh=mesh,
        in_specs=(
            P("section", "dp", "tensor"),
            P("section", None, "dp", "tensor"),
            P("section"),
            P("section", "dp", "tensor"),
            P("section", "tensor"),
            P("section", None, "tensor"),
            P("section", "tensor", None),
            P("section", "tensor", None),
        ),
        out_specs=(
            P("section", "dp", "tensor"),
            P("section", "dp", "tensor"),
            P("section", "dp", "tensor"),
        ),
        check_vma=False,
    )
```

```python
import functools

import jax
import jax.numpy as jnp
import numpy as np
from jax import lax
from jax.experimental import pallas as pl
from jax.experimental.pallas import tpu as pltpu
from jax.sharding import PartitionSpec as P

HEADS = 32
KVH = 4
HD = 128
TOK = 128
WIDTH = 4096
COLS = 256
SIDE = 4
norm_eps = 1e-05
MIB = 1024 * 1024

FIRST, SECOND = 0, 1


def tensor_rows(section, order):
    if (section + order) % 2 == 0:
        return [[x * SIDE + y for y in range(SIDE)] for x in range(SIDE)]
    return [[x * SIDE + y for x in range(SIDE)] for y in range(SIDE)]


NN = (((1,), (0,)), ((), ()))
NT = (((1,), (1,)), ((), ()))
TN = (((0,), (0,)), ((), ()))


def rope_angles():
    inverse = 10000.0 ** (-2.0 * np.arange(HD // 2, dtype=np.float64) / HD)
    angles = np.arange(TOK, dtype=np.float64)[:, None] * inverse[None, :]
    return np.cos(angles).astype(np.float32), np.sin(angles).astype(np.float32)


def matmul(left, right, dims):
    return lax.dot_general(left, right, dims, preferred_element_type=jnp.float32)


def exchange(blocks, order):
    sections = range(lax.axis_size("section"))
    groups = [[s * 16 + t for t in row] for s in sections for row in tensor_rows(s, order)]
    return lax.all_to_all(blocks, ("section", "tensor"), 0, 0, axis_index_groups=groups)


def exchange_heads(blocks):
    return lax.all_to_all(blocks, "tensor", 0, 0, axis_index_groups=tensor_rows(0, FIRST))


def call(kernel, outs, *operands, vmem=32, flops=0):
    nbytes = sum(int(np.prod(a.shape)) * a.dtype.itemsize for a in (*operands, *outs))
    specs = [
        pl.BlockSpec(memory_space=pltpu.SMEM if a.shape == (3,) else pltpu.VMEM) for a in operands
    ]
    return pl.pallas_call(
        kernel,
        out_shape=outs,
        in_specs=specs,
        compiler_params=pltpu.CompilerParams(vmem_limit_bytes=vmem * MIB),
        cost_estimate=pl.CostEstimate(flops=flops, bytes_accessed=nbytes, transcendentals=0),
    )(*operands)


def shape(dims, dtype=jnp.bfloat16):
    return jax.ShapeDtypeStruct(dims, dtype)


def block_index(pos_ref, k, j):
    return k * pos_ref[0] + j * pos_ref[1]


def weight_rows(t):
    return pl.ds(pl.multiple_of(t * COLS, COLS), COLS)


def pack_kv_weight(pos_ref, w_ref, out_ref):
    swapped = pos_ref[1] > 1
    for x in range(SIDE):
        keys = w_ref[:, x * HD : (x + 1) * HD].T
        values = w_ref[:, (KVH + x) * HD : (KVH + x + 1) * HD].T
        for y in range(SIDE):
            k, j = jnp.where(swapped, y, x), jnp.where(swapped, x, y)
            out_ref[k, j, 0:16] = keys[16 * y : 16 * y + 16]
            out_ref[k, j, 16:32] = keys[64 + 16 * y : 80 + 16 * y]
            out_ref[k, j, 32:64] = values[32 * y : 32 * y + 32]


def first_blocks(rows_ref, back_ref, cot_ref, gain_ref, kvw_ref, out_ref):
    gain = gain_ref[...]
    row = lax.broadcasted_iota(jnp.int32, (16, COLS), 0)
    high = gain.astype(jnp.bfloat16).astype(jnp.float32)
    middle = (gain - high).astype(jnp.bfloat16).astype(jnp.float32)
    low = gain - high - middle
    gains = jnp.where(row == 0, high, jnp.where(row == 1, middle, jnp.where(row == 2, low, 0.0)))
    for j in range(SIDE):
        out_ref[j, 0:TOK] = rows_ref[...]
        out_ref[j, TOK : 2 * TOK] = back_ref[...]
        out_ref[j, 2 * TOK : 3 * TOK] = cot_ref[...]
        out_ref[j, 384:400] = gains.astype(jnp.bfloat16)
        for k in range(SIDE):
            out_ref[j, 400 + 64 * k : 464 + 64 * k] = kvw_ref[k, j]


def second_blocks(parts_ref, out_ref):
    row = lax.broadcasted_iota(jnp.int32, (16, COLS), 0)
    gains = jnp.zeros((16, COLS), jnp.float32)
    for j in range(SIDE):
        part = parts_ref[j, 384:400].astype(jnp.float32)
        for i in range(3):
            gains = jnp.where(row == 3 * j + i, part[i : i + 1], gains)
    gains = gains.astype(jnp.bfloat16)
    for k in range(SIDE):
        for j in range(SIDE):
            out_ref[k, j * 384 : (j + 1) * 384] = parts_ref[j, 0:384]
        out_ref[k, 1536:1552] = gains


def norm_and_kv(pos_ref, rows_ref, first_ref, table_ref, normed_ref, kv_ref, raw_ref, factor_ref):
    total = jnp.zeros((2 * TOK, COLS), jnp.float32)
    for k in range(SIDE):
        for j in range(SIDE):
            block = rows_ref[k, j * 384 : j * 384 + 256].astype(jnp.float32)
            total = total + block * block
    factor = lax.rsqrt(jnp.sum(total, axis=1, keepdims=True) / WIDTH + norm_eps)
    factor_ref[...] = jnp.broadcast_to(factor[TOK:], (TOK, HD))
    kv = jnp.zeros((64, 2 * TOK), jnp.float32)
    for k in range(SIDE):
        gains = rows_ref[k, 1536:1552].astype(jnp.float32)
        for j in range(SIDE):
            gain = gains[3 * j : 3 * j + 1] + gains[3 * j + 1 : 3 * j + 2] + gains[3 * j + 2 : 3 * j + 3]
            block = rows_ref[k, j * 384 : j * 384 + 256].astype(jnp.float32)
            normed = (block * factor * gain).astype(jnp.bfloat16)
            normed_ref[k * SIDE + j] = normed
            kv = kv + matmul(first_ref[j, 400 + 64 * k : 464 + 64 * k], normed, NT)
    raw_ref[...] = kv[:, TOK:]
    first, second = kv[0:16], kv[16:32]
    start = pl.multiple_of(pos_ref[2] * 16, 16)
    cos, sin = table_ref[pl.ds(256 + start, 16)], table_ref[pl.ds(320 + start, 16)]
    cos, sin = jnp.concatenate([cos, cos], axis=1), jnp.concatenate([sin, sin], axis=1)
    out = jnp.concatenate([first * cos - second * sin, second * cos + first * sin, kv[32:64]], axis=0)
    out = out.astype(jnp.bfloat16)
    for y in range(SIDE):
        kv_ref[y] = out


def attention(
    pos_ref, rows_ref, normed_ref, kv_ref, qw_ref, ow_ref, table_ref,
    attended_ref, grad_query_ref, grad_kv_ref, mixed_ref,
):
    query = jnp.zeros((2 * TOK, COLS), jnp.float32)
    grad_out = jnp.zeros((TOK, COLS), jnp.float32)
    for k in range(SIDE):
        for j in range(SIDE):
            block = weight_rows(block_index(pos_ref, k, j))
            query = query + matmul(normed_ref[k * SIDE + j], qw_ref[block, :], NN)
            cot = rows_ref[k, j * 384 + 256 : j * 384 + 384]
            grad_out = grad_out + matmul(cot, ow_ref[:, block], NT)
    grad_out = grad_out.astype(jnp.bfloat16)
    kv = [kv_ref[y] for y in range(SIDE)]
    cos, sin = table_ref[0:128], table_ref[128:256]
    scale = HD ** (-0.5)
    causal = lax.broadcasted_iota(jnp.int32, (TOK, TOK), 0) >= lax.broadcasted_iota(
        jnp.int32, (TOK, TOK), 1
    )

    def softmax(scores):
        scores = jnp.where(causal, scores, -1e30)
        shifted = jnp.exp(scores - jnp.max(scores, axis=-1, keepdims=True))
        return shifted / jnp.sum(shifted, axis=-1, keepdims=True)

    def keys_values(start):
        part = [k[:, start : start + TOK] for k in kv]
        keys = jnp.concatenate([p[0:16] for p in part] + [p[16:32] for p in part], axis=0)
        return keys, jnp.concatenate([p[32:64] for p in part], axis=0)

    def heads(start, h):
        raw = query[start : start + TOK, h * HD : (h + 1) * HD]
        turned = raw * cos + pltpu.roll(raw, HD // 2, 1) * sin
        return raw, (turned * scale).astype(jnp.bfloat16)

    keys, values = keys_values(0)
    for h in range(2):
        _, query_head = heads(0, h)
        weights = softmax(matmul(query_head, keys, NN)).astype(jnp.bfloat16)
        attended_ref[:, h * HD : (h + 1) * HD] = matmul(weights, values, NT).astype(jnp.bfloat16)

    keys, values = keys_values(TOK)
    grad_key = jnp.zeros((HD, TOK), jnp.float32)
    grad_value = jnp.zeros((HD, TOK), jnp.float32)
    mixed = jnp.zeros((TOK, HD), jnp.float32)
    for h in range(2):
        raw, query_head = heads(TOK, h)
        probs = softmax(matmul(query_head, keys, NN))
        grad_head = grad_out[:, h * HD : (h + 1) * HD]
        grad_probs = matmul(grad_head, values, NN)
        delta = jnp.sum(probs * grad_probs, axis=-1, keepdims=True)
        grad_scores = (probs * (grad_probs - delta)).astype(jnp.bfloat16)
        turned = matmul(grad_scores, keys, NT)
        grad_query = (turned * cos - pltpu.roll(turned, HD // 2, 1) * sin) * scale
        grad_query = grad_query.astype(jnp.bfloat16)
        grad_query_ref[:, h * HD : (h + 1) * HD] = grad_query
        mixed = mixed + grad_query.astype(jnp.float32) * raw
        grad_key = grad_key + matmul(query_head, grad_scores, TN)
        grad_value = grad_value + matmul(grad_head, probs.astype(jnp.bfloat16), TN)
    cost, sint = table_ref[256:320], table_ref[320:384]
    first, second = grad_key[:64], grad_key[64:]
    key_first = first * cost + second * sint
    key_second = second * cost - first * sint
    for y in range(SIDE):
        grad_kv_ref[y, 0:16] = key_first[16 * y : 16 * y + 16]
        grad_kv_ref[y, 16:32] = key_second[16 * y : 16 * y + 16]
        grad_kv_ref[y, 32:64] = grad_value[32 * y : 32 * y + 32]
    mixed_ref[...] = jnp.broadcast_to(jnp.sum(mixed.T, axis=0, keepdims=True), (8, TOK))


def split_rows(total):
    high = total.astype(jnp.bfloat16)
    low = (total - high.astype(jnp.float32)).astype(jnp.bfloat16)
    row = lax.broadcasted_iota(jnp.int32, (16, TOK), 0)
    both = jnp.where(row == 0, high.astype(jnp.float32), low.astype(jnp.float32))
    both = jnp.where(row < 2, both, 0.0)
    return jnp.concatenate([both, jnp.zeros((16, COLS - TOK), jnp.float32)], axis=1).astype(jnp.bfloat16)


def project(
    pos_ref, attended_ref, grad_query_ref, grad_kv_ref, raw_ref, mixed_ref, qw_ref, ow_ref, first_ref, out_ref
):
    attended = attended_ref[...]
    grad_query = grad_query_ref[...]
    grad_kv = grad_kv_ref[0] + grad_kv_ref[1] + grad_kv_ref[2] + grad_kv_ref[3]
    grad_kv = grad_kv.astype(jnp.bfloat16)
    mixed = mixed_ref[0:1] + jnp.sum(grad_kv.astype(jnp.float32) * raw_ref[...], axis=0, keepdims=True)
    rows = split_rows(mixed)
    for k in range(SIDE):
        for j in range(SIDE):
            block = weight_rows(block_index(pos_ref, k, j))
            term = matmul(attended, ow_ref[:, block], NN)
            out_ref[k, j * 256 : j * 256 + TOK] = term.astype(jnp.bfloat16)
            term = matmul(grad_query, qw_ref[block, :], NT)
            term = term + matmul(grad_kv, first_ref[j, 400 + 64 * k : 464 + 64 * k], TN)
            out_ref[k, j * 256 + TOK : j * 256 + 256] = term.astype(jnp.bfloat16)
        out_ref[k, 1024:1040] = rows


def sum_second(parts_ref, out_ref):
    rows = jnp.zeros((16, COLS), jnp.float32)
    for k in range(SIDE):
        rows = rows + parts_ref[k, 1024:1040].astype(jnp.float32)
    mixed = split_rows(rows[0:1, :TOK] + rows[1:2, :TOK])
    for j in range(SIDE):
        total = jnp.zeros((256, COLS), jnp.float32)
        for k in range(SIDE):
            total = total + parts_ref[k, j * 256 : j * 256 + 256].astype(jnp.float32)
        out_ref[j, 0:256] = total.astype(jnp.bfloat16)
        out_ref[j, 256:272] = mixed


def finish(parts_ref, rows_ref, back_ref, cot_ref, gain_ref, factor_ref, out_ref, grad_ref):
    total = parts_ref[0].astype(jnp.float32)
    for j in range(1, SIDE):
        total = total + parts_ref[j].astype(jnp.float32)
    out_ref[...] = (rows_ref[...].astype(jnp.float32) + total[0:TOK]).astype(jnp.bfloat16)
    mixed = jnp.broadcast_to(total[256:257, :TOK] + total[257:258, :TOK], (TOK, TOK)).T[:, 0:1]
    factor = factor_ref[:, 0:1]
    scaled = total[TOK : 2 * TOK] * gain_ref[...]
    grad_rows = factor * scaled - back_ref[...].astype(jnp.float32) * (factor * factor * mixed / WIDTH)
    grad_ref[...] = (cot_ref[...].astype(jnp.float32) + grad_rows).astype(jnp.bfloat16)


def per_device(
    section_input,
    stash_pool,
    reload_slot,
    cotangent,
    norm_gain,
    query_weight,
    kv_weight,
    out_weight,
):
    token_rows = section_input[0]
    cot_rows = cotangent[0]
    query_w = query_weight[0]
    kv_w = kv_weight[0]
    out_w = out_weight[0]
    section_count = lax.axis_size("section")
    section_pos = lax.axis_index("section")
    is_early = section_pos < section_count // 2

    picked = lax.dynamic_index_in_dim(stash_pool[0], reload_slot[0], 0, keepdims=False)
    sending = jnp.where(is_early, token_rows, picked)
    mirrored = [(s, section_count - 1 - s) for s in range(section_count)]
    received = lax.ppermute(sending, "section", mirrored)
    back_rows = jnp.where(is_early, received, token_rows)

    tensor_pos = lax.axis_index("tensor").astype(jnp.int32)
    odd = (section_pos % 2).astype(jnp.int32)
    pos = jnp.stack([SIDE - 3 * odd, 1 + 3 * odd, tensor_pos % SIDE])
    cos, sin = rope_angles()
    wide = np.concatenate([cos, cos], axis=1), np.concatenate([-sin, sin], axis=1)
    table = jnp.asarray(np.concatenate([*wide, cos.T, sin.T], axis=0))

    packed = call(pack_kv_weight, (shape((SIDE, SIDE, 64, COLS)),), pos, kv_w)[0]
    packed = exchange(packed, SECOND)
    gain_row = norm_gain
    blocks = call(
        first_blocks, (shape((SIDE, 656, COLS)),), token_rows, back_rows, cot_rows, gain_row, packed
    )[0]
    first = exchange(blocks, FIRST)
    blocks = call(second_blocks, (shape((SIDE, 1552, COLS)),), first)[0]
    rows = exchange(blocks, SECOND)

    normed, kv_own, kv_raw, factor = call(
        norm_and_kv,
        (
            shape((16, 2 * TOK, COLS)),
            shape((SIDE, 64, 2 * TOK)),
            shape((64, TOK), jnp.float32),
            shape((TOK, HD), jnp.float32),
        ),
        pos, rows, first, table,
        flops=2 * 64 * 256 * 4096,
    )
    kv_all = exchange_heads(kv_own)
    attended, grad_query, grad_kv, mixed = call(
        attention,
        (
            shape((TOK, COLS)),
            shape((TOK, COLS)),
            shape((SIDE, 64, TOK), jnp.float32),
            shape((8, TOK), jnp.float32),
        ),
        pos, rows, normed, kv_all, query_w, out_w, table,
        flops=2 * 384 * 256 * 4096,
    )
    grad_kv = exchange_heads(grad_kv)
    terms = call(
        project,
        (shape((SIDE, 1040, COLS)),),
        pos, attended, grad_query, grad_kv, kv_raw, mixed, query_w, out_w, first,
        flops=2 * 256 * 256 * 4096,
    )[0]
    terms = exchange(terms, SECOND)
    terms = call(sum_second, (shape((SIDE, 272, COLS)),), terms)[0]
    terms = exchange(terms, FIRST)
    layer_out, grad_local = call(
        finish,
        (shape((TOK, COLS)), shape((TOK, COLS))),
        terms, token_rows, back_rows, cot_rows, gain_row, factor,
    )
    next_input = lax.ppermute(layer_out, "section", [(s, s + 1) for s in range(section_count - 1)])
    input_grad = lax.ppermute(grad_local, "section", [(s + 1, s) for s in range(section_count - 1)])
    return (next_input[None], received[None], input_grad[None])


def solution(mesh):
    return jax.shard_map(
        per_device,
        mesh=mesh,
        in_specs=(
            P("section", "dp", "tensor"),
            P("section", None, "dp", "tensor"),
            P("section"),
            P("section", "dp", "tensor"),
            P("section", "tensor"),
            P("section", None, "tensor"),
            P("section", "tensor", None),
            P("section", "tensor", None),
        ),
        out_specs=(
            P("section", "dp", "tensor"),
            P("section", "dp", "tensor"),
            P("section", "dp", "tensor"),
        ),
        check_vma=False,
    )
```

```python
import functools

import jax
import jax.numpy as jnp
import numpy as np
from jax import lax
from jax.experimental import pallas as pl
from jax.experimental.pallas import tpu as pltpu
from jax.sharding import PartitionSpec as P

HEADS = 32
KVH = 4
HD = 128
TOK = 128
WIDTH = 4096
COLS = 256
SIDE = 4
norm_eps = 1e-05
MIB = 1024 * 1024

FIRST, SECOND = 0, 1


def tensor_rows(section, order):
    if (section + order) % 2 == 0:
        return [[x * SIDE + y for y in range(SIDE)] for x in range(SIDE)]
    return [[x * SIDE + y for x in range(SIDE)] for y in range(SIDE)]


NN = (((1,), (0,)), ((), ()))
NT = (((1,), (1,)), ((), ()))
TN = (((0,), (0,)), ((), ()))


def rope_angles():
    inverse = 10000.0 ** (-2.0 * np.arange(HD // 2, dtype=np.float64) / HD)
    angles = np.arange(TOK, dtype=np.float64)[:, None] * inverse[None, :]
    return np.cos(angles).astype(np.float32), np.sin(angles).astype(np.float32)


def matmul(left, right, dims):
    return lax.dot_general(left, right, dims, preferred_element_type=jnp.float32)


def exchange(blocks, order):
    sections = range(lax.axis_size("section"))
    groups = [[s * 16 + t for t in row] for s in sections for row in tensor_rows(s, order)]
    return lax.all_to_all(blocks, ("section", "tensor"), 0, 0, axis_index_groups=groups)


def exchange_row(blocks, axis):
    return lax.all_to_all(blocks, "tensor", 0, 0, axis_index_groups=tensor_rows(1 - axis, FIRST))


def call(kernel, outs, *operands, vmem=32, flops=0, scratch=(), in_place=False):
    nbytes = sum(int(np.prod(a.shape)) * a.dtype.itemsize for a in (*operands, *outs))
    spaces = [
        pltpu.SMEM if a.shape == (3,) else pltpu.HBM if in_place else pltpu.VMEM for a in operands
    ]
    return pl.pallas_call(
        kernel,
        out_shape=outs,
        in_specs=[pl.BlockSpec(memory_space=space) for space in spaces],
        scratch_shapes=scratch,
        compiler_params=pltpu.CompilerParams(vmem_limit_bytes=vmem * MIB),
        cost_estimate=pl.CostEstimate(flops=flops, bytes_accessed=nbytes, transcendentals=0),
    )(*operands)


def shape(dims, dtype=jnp.bfloat16):
    return jax.ShapeDtypeStruct(dims, dtype)


def block_index(pos_ref, k, j):
    return k * pos_ref[0] + j * pos_ref[1]


def weight_rows(t):
    return pl.ds(pl.multiple_of(t * COLS, COLS), COLS)


def first_blocks(pos_ref, *refs):
    sources, out_ref, (rows_ref, cot_ref, gain_ref, kvw_ref), sems = refs[:4], refs[4], refs[5:9], refs[9]
    held = (rows_ref, cot_ref, gain_ref, kvw_ref)
    copies = [pltpu.make_async_copy(a, b, sems.at[n]) for n, (a, b) in enumerate(zip(sources, held))]
    for copy in copies:
        copy.start()
    for copy in copies[:3]:
        copy.wait()
    gain = gain_ref[...]
    row = lax.broadcasted_iota(jnp.int32, (16, COLS), 0)
    high = gain.astype(jnp.bfloat16).astype(jnp.float32)
    middle = (gain - high).astype(jnp.bfloat16).astype(jnp.float32)
    low = gain - high - middle
    gains = jnp.where(row == 0, high, jnp.where(row == 1, middle, jnp.where(row == 2, low, 0.0)))
    for j in range(SIDE):
        out_ref[j, 0:TOK] = rows_ref[...]
        out_ref[j, TOK : 2 * TOK] = cot_ref[...]
        out_ref[j, 256:272] = gains.astype(jnp.bfloat16)
    copies[3].wait()
    swapped = pos_ref[1] > 1
    for x in range(SIDE):
        keys = kvw_ref[:, x * HD : (x + 1) * HD].T
        values = kvw_ref[:, (KVH + x) * HD : (KVH + x + 1) * HD].T
        for y in range(SIDE):
            k, j = jnp.where(swapped, y, x), jnp.where(swapped, x, y)
            start = pl.multiple_of(272 + 64 * k, 16)
            out_ref[j, pl.ds(start, 16)] = keys[16 * y : 16 * y + 16]
            out_ref[j, pl.ds(start + 16, 16)] = keys[64 + 16 * y : 80 + 16 * y]
            out_ref[j, pl.ds(start + 32, 32)] = values[32 * y : 32 * y + 32]


def second_blocks(parts_ref, back_ref, out_ref):
    row = lax.broadcasted_iota(jnp.int32, (16, COLS), 0)
    gains = jnp.zeros((16, COLS), jnp.float32)
    for j in range(SIDE):
        part = parts_ref[j, 256:272].astype(jnp.float32)
        for i in range(3):
            gains = jnp.where(row == 3 * j + i, part[i : i + 1], gains)
    gains = gains.astype(jnp.bfloat16)
    for k in range(SIDE):
        for j in range(SIDE):
            out_ref[k, j * 256 : (j + 1) * 256] = parts_ref[j, 0:256]
            out_ref[k, 1040 + 64 * j : 1104 + 64 * j] = parts_ref[j, 272 + 64 * k : 336 + 64 * k]
        out_ref[k, 1024:1040] = gains
        out_ref[k, 1296:1424] = back_ref[...]


def third_blocks(parts_ref, out_ref):
    for j in range(SIDE):
        for k in range(SIDE):
            out_ref[j, k * TOK : (k + 1) * TOK] = parts_ref[k, 1296:1424]


def deliver(out_ref, grad_ref, received_ref, next_ref, before_ref, copy_ref):
    next_ref[...] = out_ref[...]
    before_ref[...] = grad_ref[...]
    copy_ref[...] = received_ref[...]


def norm_and_kv(pos_ref, rows_ref, back_ref, table_ref, normed_ref, kv_ref, raw_ref, factor_ref):
    def blocks(k, j):
        block = rows_ref[k, j * 256 : j * 256 + TOK].astype(jnp.float32)
        return block, back_ref[j, k * TOK : (k + 1) * TOK].astype(jnp.float32)

    total = jnp.zeros((TOK, COLS), jnp.float32)
    back_total = jnp.zeros((TOK, COLS), jnp.float32)
    for k in range(SIDE):
        for j in range(SIDE):
            block, back_block = blocks(k, j)
            total = total + block * block
            back_total = back_total + back_block * back_block
    factor = lax.rsqrt(jnp.sum(total, axis=1, keepdims=True) / WIDTH + norm_eps)
    back_factor = lax.rsqrt(jnp.sum(back_total, axis=1, keepdims=True) / WIDTH + norm_eps)
    factor_ref[...] = jnp.broadcast_to(back_factor, (TOK, HD))
    kv = jnp.zeros((64, 2 * TOK), jnp.float32)
    for k in range(SIDE):
        gains = rows_ref[k, 1024:1040].astype(jnp.float32)
        for j in range(SIDE):
            gain = gains[3 * j : 3 * j + 1] + gains[3 * j + 1 : 3 * j + 2] + gains[3 * j + 2 : 3 * j + 3]
            block, back_block = blocks(k, j)
            normed_ref[k * SIDE + j, 0:TOK] = (block * factor * gain).astype(jnp.bfloat16)
            normed_ref[k * SIDE + j, TOK:] = (back_block * back_factor * gain).astype(jnp.bfloat16)
            weight = rows_ref[k, 1040 + 64 * j : 1104 + 64 * j]
            kv = kv + matmul(weight, normed_ref[k * SIDE + j], NT)
    raw_ref[...] = kv[:, TOK:]
    first, second = kv[0:16], kv[16:32]
    start = pl.multiple_of(pos_ref[2] * 16, 16)
    cos, sin = table_ref[pl.ds(256 + start, 16)], table_ref[pl.ds(320 + start, 16)]
    cos, sin = jnp.concatenate([cos, cos], axis=1), jnp.concatenate([sin, sin], axis=1)
    out = jnp.concatenate([first * cos - second * sin, second * cos + first * sin, kv[32:64]], axis=0)
    out = out.astype(jnp.bfloat16)
    for y in range(SIDE):
        kv_ref[y] = out


def attention(
    pos_ref, rows_ref, normed_ref, kv_ref, qw_ref, ow_ref, table_ref,
    attended_ref, grad_query_ref, grad_kv_ref, mixed_ref,
):
    query = jnp.zeros((2 * TOK, COLS), jnp.float32)
    grad_out = jnp.zeros((TOK, COLS), jnp.float32)
    for k in range(SIDE):
        for j in range(SIDE):
            block = weight_rows(block_index(pos_ref, k, j))
            query = query + matmul(normed_ref[k * SIDE + j], qw_ref[block, :], NN)
            cot = rows_ref[k, j * 256 + TOK : (j + 1) * 256]
            grad_out = grad_out + matmul(cot, ow_ref[:, block], NT)
    grad_out = grad_out.astype(jnp.bfloat16)
    kv = [kv_ref[y] for y in range(SIDE)]
    cos, sin = table_ref[0:128], table_ref[128:256]
    scale = HD ** (-0.5)
    causal = lax.broadcasted_iota(jnp.int32, (TOK, TOK), 0) >= lax.broadcasted_iota(
        jnp.int32, (TOK, TOK), 1
    )

    def softmax(scores):
        scores = jnp.where(causal, scores, -1e30)
        shifted = jnp.exp(scores - jnp.max(scores, axis=-1, keepdims=True))
        return shifted / jnp.sum(shifted, axis=-1, keepdims=True)

    def keys_values(start):
        part = [k[:, start : start + TOK] for k in kv]
        keys = jnp.concatenate([p[0:16] for p in part] + [p[16:32] for p in part], axis=0)
        return keys, jnp.concatenate([p[32:64] for p in part], axis=0)

    def heads(start, h):
        raw = query[start : start + TOK, h * HD : (h + 1) * HD]
        turned = raw * cos + pltpu.roll(raw, HD // 2, 1) * sin
        return raw, (turned * scale).astype(jnp.bfloat16)

    keys, values = keys_values(0)
    for h in range(2):
        _, query_head = heads(0, h)
        weights = softmax(matmul(query_head, keys, NN)).astype(jnp.bfloat16)
        attended_ref[:, h * HD : (h + 1) * HD] = matmul(weights, values, NT).astype(jnp.bfloat16)

    keys, values = keys_values(TOK)
    grad_key = jnp.zeros((HD, TOK), jnp.float32)
    grad_value = jnp.zeros((HD, TOK), jnp.float32)
    mixed = jnp.zeros((TOK, HD), jnp.float32)
    for h in range(2):
        raw, query_head = heads(TOK, h)
        probs = softmax(matmul(query_head, keys, NN))
        grad_head = grad_out[:, h * HD : (h + 1) * HD]
        grad_probs = matmul(grad_head, values, NN)
        delta = jnp.sum(probs * grad_probs, axis=-1, keepdims=True)
        grad_scores = (probs * (grad_probs - delta)).astype(jnp.bfloat16)
        turned = matmul(grad_scores, keys, NT)
        grad_query = (turned * cos - pltpu.roll(turned, HD // 2, 1) * sin) * scale
        grad_query = grad_query.astype(jnp.bfloat16)
        grad_query_ref[:, h * HD : (h + 1) * HD] = grad_query
        mixed = mixed + grad_query.astype(jnp.float32) * raw
        grad_key = grad_key + matmul(query_head, grad_scores, TN)
        grad_value = grad_value + matmul(grad_head, probs.astype(jnp.bfloat16), TN)
    cost, sint = table_ref[256:320], table_ref[320:384]
    first, second = grad_key[:64], grad_key[64:]
    key_first = first * cost + second * sint
    key_second = second * cost - first * sint
    for y in range(SIDE):
        grad_kv_ref[y, 0:16] = key_first[16 * y : 16 * y + 16]
        grad_kv_ref[y, 16:32] = key_second[16 * y : 16 * y + 16]
        grad_kv_ref[y, 32:64] = grad_value[32 * y : 32 * y + 32]
    mixed_ref[...] = jnp.broadcast_to(jnp.sum(mixed.T, axis=0, keepdims=True), (8, TOK))


def split_rows(total):
    high = total.astype(jnp.bfloat16)
    low = (total - high.astype(jnp.float32)).astype(jnp.bfloat16)
    row = lax.broadcasted_iota(jnp.int32, (16, TOK), 0)
    both = jnp.where(row == 0, high.astype(jnp.float32), low.astype(jnp.float32))
    both = jnp.where(row < 2, both, 0.0)
    return jnp.concatenate([both, jnp.zeros((16, COLS - TOK), jnp.float32)], axis=1).astype(jnp.bfloat16)


def project(
    pos_ref, attended_ref, grad_query_ref, grad_kv_ref, raw_ref, mixed_ref, qw_ref, ow_ref, rows_ref, out_ref
):
    attended = attended_ref[...]
    grad_query = grad_query_ref[...]
    grad_kv = grad_kv_ref[0] + grad_kv_ref[1] + grad_kv_ref[2] + grad_kv_ref[3]
    grad_kv = grad_kv.astype(jnp.bfloat16)
    mixed = mixed_ref[0:1] + jnp.sum(grad_kv.astype(jnp.float32) * raw_ref[...], axis=0, keepdims=True)
    rows = split_rows(mixed)
    for k in range(SIDE):
        for j in range(SIDE):
            t = block_index(pos_ref, k, j)
            block = weight_rows(t)
            start = pl.multiple_of(lax.rem(t, SIDE) * 256, 256)
            term = matmul(attended, ow_ref[:, block], NN)
            out_ref[lax.div(t, SIDE), pl.ds(start, TOK)] = term.astype(jnp.bfloat16)
            term = matmul(grad_query, qw_ref[block, :], NT)
            term = term + matmul(grad_kv, rows_ref[k, 1040 + 64 * j : 1104 + 64 * j], TN)
            out_ref[lax.div(t, SIDE), pl.ds(start + TOK, TOK)] = term.astype(jnp.bfloat16)
    for x in range(SIDE):
        out_ref[x, 1024:1040] = rows


def sum_first(parts_ref, out_ref):
    rows = jnp.zeros((16, COLS), jnp.float32)
    for k in range(SIDE):
        rows = rows + parts_ref[k, 1024:1040].astype(jnp.float32)
    mixed = split_rows(rows[0:1, :TOK] + rows[1:2, :TOK])
    for j in range(SIDE):
        total = jnp.zeros((256, COLS), jnp.float32)
        for k in range(SIDE):
            total = total + parts_ref[k, j * 256 : j * 256 + 256].astype(jnp.float32)
        out_ref[j, 0:256] = total.astype(jnp.bfloat16)
        out_ref[j, 256:272] = mixed


def finish(parts_ref, rows_ref, back_ref, cot_ref, gain_ref, factor_ref, out_ref, grad_ref):
    total = parts_ref[0].astype(jnp.float32)
    for j in range(1, SIDE):
        total = total + parts_ref[j].astype(jnp.float32)
    out_ref[...] = (rows_ref[...].astype(jnp.float32) + total[0:TOK]).astype(jnp.bfloat16)
    mixed = jnp.broadcast_to(total[256:257, :TOK] + total[257:258, :TOK], (TOK, TOK)).T[:, 0:1]
    factor = factor_ref[:, 0:1]
    scaled = total[TOK : 2 * TOK] * gain_ref[...]
    grad_rows = factor * scaled - back_ref[...].astype(jnp.float32) * (factor * factor * mixed / WIDTH)
    grad_ref[...] = (cot_ref[...].astype(jnp.float32) + grad_rows).astype(jnp.bfloat16)


def per_device(
    section_input,
    stash_pool,
    reload_slot,
    cotangent,
    norm_gain,
    query_weight,
    kv_weight,
    out_weight,
):
    token_rows = section_input[0]
    cot_rows = cotangent[0]
    query_w = query_weight[0]
    kv_w = kv_weight[0]
    out_w = out_weight[0]
    section_count = lax.axis_size("section")
    section_pos = lax.axis_index("section")
    is_early = section_pos < section_count // 2

    picked = lax.dynamic_index_in_dim(stash_pool[0], reload_slot[0], 0, keepdims=False)
    sending = jnp.where(is_early, token_rows, picked)
    mirrored = [(s, section_count - 1 - s) for s in range(section_count)]
    received = lax.ppermute(sending, "section", mirrored)
    back_rows = jnp.where(is_early, received, token_rows)

    tensor_pos = lax.axis_index("tensor").astype(jnp.int32)
    odd = (section_pos % 2).astype(jnp.int32)
    pos = jnp.stack([SIDE - 3 * odd, 1 + 3 * odd, tensor_pos % SIDE])
    cos, sin = rope_angles()
    wide = np.concatenate([cos, cos], axis=1), np.concatenate([-sin, sin], axis=1)
    table = jnp.asarray(np.concatenate([*wide, cos.T, sin.T], axis=0))
    gain_row = norm_gain

    held = [pltpu.VMEM(a.shape, a.dtype) for a in (token_rows, cot_rows, gain_row, kv_w)]
    blocks = call(
        first_blocks,
        (shape((SIDE, 528, COLS)),),
        pos, token_rows, cot_rows, gain_row, kv_w,
        scratch=(*held, pltpu.SemaphoreType.DMA((4,))),
        in_place=True,
        vmem=58,
    )[0]
    blocks = exchange(blocks, FIRST)
    blocks = call(second_blocks, (shape((SIDE, 1424, COLS)),), blocks, back_rows)[0]
    rows = exchange(blocks, SECOND)
    blocks = call(third_blocks, (shape((SIDE, 4 * TOK, COLS)),), rows)[0]
    back = exchange(blocks, FIRST)

    normed, kv_own, kv_raw, factor = call(
        norm_and_kv,
        (
            shape((16, 2 * TOK, COLS)),
            shape((SIDE, 64, 2 * TOK)),
            shape((64, TOK), jnp.float32),
            shape((TOK, HD), jnp.float32),
        ),
        pos, rows, back, table,
        flops=2 * 64 * 256 * 4096,
    )
    kv_all = exchange_row(kv_own, 1)
    attended, grad_query, grad_kv, mixed = call(
        attention,
        (
            shape((TOK, COLS)),
            shape((TOK, COLS)),
            shape((SIDE, 64, TOK), jnp.float32),
            shape((8, TOK), jnp.float32),
        ),
        pos, rows, normed, kv_all, query_w, out_w, table,
        flops=2 * 384 * 256 * 4096,
    )
    grad_kv = exchange_row(grad_kv, 1)
    terms = call(
        project,
        (shape((SIDE, 1040, COLS)),),
        pos, attended, grad_query, grad_kv, kv_raw, mixed, query_w, out_w, rows,
        flops=2 * 256 * 256 * 4096,
    )[0]
    terms = exchange_row(terms, 0)
    terms = call(sum_first, (shape((SIDE, 272, COLS)),), terms)[0]
    terms = exchange_row(terms, 1)
    layer_out, grad_local = call(
        finish,
        (shape((TOK, COLS)), shape((TOK, COLS))),
        terms, token_rows, back_rows, cot_rows, gain_row, factor,
    )
    next_input = lax.ppermute(layer_out, "section", [(s, s + 1) for s in range(section_count - 1)])
    input_grad = lax.ppermute(grad_local, "section", [(s + 1, s) for s in range(section_count - 1)])
    next_input, input_grad, received = call(
        deliver, (shape((TOK, COLS)),) * 3, next_input, input_grad, received
    )
    return (next_input[None], received[None], input_grad[None])


def solution(mesh):
    return jax.shard_map(
        per_device,
        mesh=mesh,
        in_specs=(
            P("section", "dp", "tensor"),
            P("section", None, "dp", "tensor"),
            P("section"),
            P("section", "dp", "tensor"),
            P("section", "tensor"),
            P("section", None, "tensor"),
            P("section", "tensor", None),
            P("section", "tensor", None),
        ),
        out_specs=(
            P("section", "dp", "tensor"),
            P("section", "dp", "tensor"),
            P("section", "dp", "tensor"),
        ),
        check_vma=False,
    )
```

```python
import functools

import jax
import jax.numpy as jnp
import numpy as np
from jax import lax
from jax.experimental import pallas as pl
from jax.experimental.pallas import tpu as pltpu
from jax.sharding import PartitionSpec as P

HEADS = 32
KVH = 4
HD = 128
TOK = 128
WIDTH = 4096
COLS = 256
SIDE = 4
norm_eps = 1e-05
MIB = 1024 * 1024

FIRST, SECOND = 0, 1


def tensor_rows(section, order):
    if (section + order) % 2 == 0:
        return [[x * SIDE + y for y in range(SIDE)] for x in range(SIDE)]
    return [[x * SIDE + y for x in range(SIDE)] for y in range(SIDE)]


NN = (((1,), (0,)), ((), ()))
NT = (((1,), (1,)), ((), ()))
TN = (((0,), (0,)), ((), ()))


def rope_angles():
    inverse = 10000.0 ** (-2.0 * np.arange(HD // 2, dtype=np.float64) / HD)
    angles = np.arange(TOK, dtype=np.float64)[:, None] * inverse[None, :]
    return np.cos(angles).astype(np.float32), np.sin(angles).astype(np.float32)


def matmul(left, right, dims):
    return lax.dot_general(left, right, dims, preferred_element_type=jnp.float32)


def exchange(blocks, order):
    sections = range(lax.axis_size("section"))
    groups = [[s * 16 + t for t in row] for s in sections for row in tensor_rows(s, order)]
    return lax.all_to_all(blocks, ("section", "tensor"), 0, 0, axis_index_groups=groups)


def exchange_row(blocks, axis):
    return lax.all_to_all(blocks, "tensor", 0, 0, axis_index_groups=tensor_rows(1 - axis, FIRST))


def call(kernel, outs, *operands, vmem=32, flops=0, scratch=(), in_place=False):
    nbytes = sum(int(np.prod(a.shape)) * a.dtype.itemsize for a in (*operands, *outs))
    spaces = [
        pltpu.HBM if in_place else pltpu.VMEM for _ in operands
    ]
    return pl.pallas_call(
        kernel,
        out_shape=outs,
        in_specs=[pl.BlockSpec(memory_space=space) for space in spaces],
        scratch_shapes=scratch,
        compiler_params=pltpu.CompilerParams(vmem_limit_bytes=vmem * MIB),
        cost_estimate=pl.CostEstimate(flops=flops, bytes_accessed=nbytes, transcendentals=0),
    )(*operands)


def shape(dims, dtype=jnp.bfloat16):
    return jax.ShapeDtypeStruct(dims, dtype)


def position():
    section, tensor = lax.axis_index("section"), lax.axis_index("tensor")
    odd = lax.rem(section, 2)
    return SIDE - 3 * odd, 1 + 3 * odd, lax.rem(tensor, SIDE), section < lax.axis_size("section") // 2


def block_index(place, k, j):
    return k * place[0] + j * place[1]


def weight_rows(t):
    return pl.ds(pl.multiple_of(t * COLS, COLS), COLS)


def first_blocks(*refs):
    place = position()
    sources, out_ref, (rows_ref, gain_ref, kvw_ref), sems = refs[:3], refs[3], refs[4:7], refs[7]
    held = (rows_ref, gain_ref, kvw_ref)
    copies = [pltpu.make_async_copy(a, b, sems.at[n]) for n, (a, b) in enumerate(zip(sources, held))]
    for copy in copies:
        copy.start()
    for copy in copies[:2]:
        copy.wait()
    gain = gain_ref[...]
    row = lax.broadcasted_iota(jnp.int32, (16, COLS), 0)
    high = gain.astype(jnp.bfloat16).astype(jnp.float32)
    middle = (gain - high).astype(jnp.bfloat16).astype(jnp.float32)
    low = gain - high - middle
    gains = jnp.where(row == 0, high, jnp.where(row == 1, middle, jnp.where(row == 2, low, 0.0)))
    for j in range(SIDE):
        out_ref[j, 0:TOK] = rows_ref[...]
        out_ref[j, 128:144] = gains.astype(jnp.bfloat16)
    copies[2].wait()
    swapped = place[1] > 1
    for x in range(SIDE):
        keys = kvw_ref[:, x * HD : (x + 1) * HD].T
        values = kvw_ref[:, (KVH + x) * HD : (KVH + x + 1) * HD].T
        for y in range(SIDE):
            k, j = jnp.where(swapped, y, x), jnp.where(swapped, x, y)
            start = pl.multiple_of(144 + 64 * k, 16)
            out_ref[j, pl.ds(start, 16)] = keys[16 * y : 16 * y + 16]
            out_ref[j, pl.ds(start + 16, 16)] = keys[64 + 16 * y : 80 + 16 * y]
            out_ref[j, pl.ds(start + 32, 32)] = values[32 * y : 32 * y + 32]


def pick_back(reloaded_ref, rows_ref, back_ref):
    place = position()
    @pl.when(place[3])
    def _():
        back_ref[...] = reloaded_ref[...]

    @pl.when(jnp.logical_not(place[3]))
    def _():
        back_ref[...] = rows_ref[...]


def second_blocks(parts_ref, back_ref, cot_ref, out_ref):
    row = lax.broadcasted_iota(jnp.int32, (16, COLS), 0)
    gains = jnp.zeros((16, COLS), jnp.float32)
    for j in range(SIDE):
        part = parts_ref[j, 128:144].astype(jnp.float32)
        for i in range(3):
            gains = jnp.where(row == 3 * j + i, part[i : i + 1], gains)
    gains = gains.astype(jnp.bfloat16)
    for k in range(SIDE):
        for j in range(SIDE):
            out_ref[k, j * TOK : (j + 1) * TOK] = parts_ref[j, 0:TOK]
            out_ref[k, 528 + 64 * j : 592 + 64 * j] = parts_ref[j, 144 + 64 * k : 208 + 64 * k]
        out_ref[k, 512:528] = gains
        out_ref[k, 784:912] = back_ref[...]
        out_ref[k, 912:1040] = cot_ref[...]


def third_blocks(parts_ref, out_ref):
    for j in range(SIDE):
        for k in range(SIDE):
            out_ref[j, k * 256 : (k + 1) * 256] = parts_ref[k, 784:1040]


def deliver(out_ref, grad_ref, reloaded_ref, evicted_ref, next_ref, before_ref, copy_ref):
    place = position()
    next_ref[...] = out_ref[...]
    before_ref[...] = grad_ref[...]

    @pl.when(place[3])
    def _():
        copy_ref[...] = reloaded_ref[...]

    @pl.when(jnp.logical_not(place[3]))
    def _():
        copy_ref[...] = evicted_ref[...]


def norm_and_kv(rows_ref, back_ref, table_ref, normed_ref, kv_ref, raw_ref, factor_ref):
    place = position()
    def blocks(k, j):
        block = rows_ref[k, j * TOK : (j + 1) * TOK].astype(jnp.float32)
        return block, back_ref[j, k * 256 : k * 256 + TOK].astype(jnp.float32)

    total = jnp.zeros((TOK, COLS), jnp.float32)
    back_total = jnp.zeros((TOK, COLS), jnp.float32)
    for k in range(SIDE):
        for j in range(SIDE):
            block, back_block = blocks(k, j)
            total = total + block * block
            back_total = back_total + back_block * back_block
    factor = lax.rsqrt(jnp.sum(total, axis=1, keepdims=True) / WIDTH + norm_eps)
    back_factor = lax.rsqrt(jnp.sum(back_total, axis=1, keepdims=True) / WIDTH + norm_eps)
    factor_ref[...] = jnp.broadcast_to(back_factor, (TOK, HD))
    kv = jnp.zeros((64, 2 * TOK), jnp.float32)
    for k in range(SIDE):
        gains = rows_ref[k, 512:528].astype(jnp.float32)
        for j in range(SIDE):
            gain = gains[3 * j : 3 * j + 1] + gains[3 * j + 1 : 3 * j + 2] + gains[3 * j + 2 : 3 * j + 3]
            block, back_block = blocks(k, j)
            normed_ref[k * SIDE + j, 0:TOK] = (block * factor * gain).astype(jnp.bfloat16)
            normed_ref[k * SIDE + j, TOK:] = (back_block * back_factor * gain).astype(jnp.bfloat16)
            weight = rows_ref[k, 528 + 64 * j : 592 + 64 * j]
            kv = kv + matmul(weight, normed_ref[k * SIDE + j], NT)
    raw_ref[...] = kv[:, TOK:]
    first, second = kv[0:16], kv[16:32]
    start = pl.multiple_of(place[2] * 16, 16)
    cos, sin = table_ref[pl.ds(256 + start, 16)], table_ref[pl.ds(320 + start, 16)]
    cos, sin = jnp.concatenate([cos, cos], axis=1), jnp.concatenate([sin, sin], axis=1)
    out = jnp.concatenate([first * cos - second * sin, second * cos + first * sin, kv[32:64]], axis=0)
    out = out.astype(jnp.bfloat16)
    for y in range(SIDE):
        kv_ref[y] = out


def attention(
    back_ref, normed_ref, kv_ref, qw_ref, ow_ref, table_ref,
    attended_ref, grad_query_ref, grad_kv_ref, mixed_ref,
):
    place = position()
    query = jnp.zeros((2 * TOK, COLS), jnp.float32)
    grad_out = jnp.zeros((TOK, COLS), jnp.float32)
    for k in range(SIDE):
        for j in range(SIDE):
            block = weight_rows(block_index(place, k, j))
            query = query + matmul(normed_ref[k * SIDE + j], qw_ref[block, :], NN)
            cot = back_ref[j, k * 256 + TOK : (k + 1) * 256]
            grad_out = grad_out + matmul(cot, ow_ref[:, block], NT)
    grad_out = grad_out.astype(jnp.bfloat16)
    kv = [kv_ref[y] for y in range(SIDE)]
    cos, sin = table_ref[0:128], table_ref[128:256]
    scale = HD ** (-0.5)
    causal = lax.broadcasted_iota(jnp.int32, (TOK, TOK), 0) >= lax.broadcasted_iota(
        jnp.int32, (TOK, TOK), 1
    )

    def softmax(scores):
        scores = jnp.where(causal, scores, -1e30)
        shifted = jnp.exp(scores - jnp.max(scores, axis=-1, keepdims=True))
        return shifted / jnp.sum(shifted, axis=-1, keepdims=True)

    def keys_values(start):
        part = [k[:, start : start + TOK] for k in kv]
        keys = jnp.concatenate([p[0:16] for p in part] + [p[16:32] for p in part], axis=0)
        return keys, jnp.concatenate([p[32:64] for p in part], axis=0)

    def heads(start, h):
        raw = query[start : start + TOK, h * HD : (h + 1) * HD]
        turned = raw * cos + pltpu.roll(raw, HD // 2, 1) * sin
        return raw, (turned * scale).astype(jnp.bfloat16)

    keys, values = keys_values(0)
    for h in range(2):
        _, query_head = heads(0, h)
        weights = softmax(matmul(query_head, keys, NN)).astype(jnp.bfloat16)
        attended_ref[:, h * HD : (h + 1) * HD] = matmul(weights, values, NT).astype(jnp.bfloat16)

    keys, values = keys_values(TOK)
    grad_key = jnp.zeros((HD, TOK), jnp.float32)
    grad_value = jnp.zeros((HD, TOK), jnp.float32)
    mixed = jnp.zeros((TOK, HD), jnp.float32)
    for h in range(2):
        raw, query_head = heads(TOK, h)
        probs = softmax(matmul(query_head, keys, NN))
        grad_head = grad_out[:, h * HD : (h + 1) * HD]
        grad_probs = matmul(grad_head, values, NN)
        delta = jnp.sum(probs * grad_probs, axis=-1, keepdims=True)
        grad_scores = (probs * (grad_probs - delta)).astype(jnp.bfloat16)
        turned = matmul(grad_scores, keys, NT)
        grad_query = (turned * cos - pltpu.roll(turned, HD // 2, 1) * sin) * scale
        grad_query = grad_query.astype(jnp.bfloat16)
        grad_query_ref[:, h * HD : (h + 1) * HD] = grad_query
        mixed = mixed + grad_query.astype(jnp.float32) * raw
        grad_key = grad_key + matmul(query_head, grad_scores, TN)
        grad_value = grad_value + matmul(grad_head, probs.astype(jnp.bfloat16), TN)
    cost, sint = table_ref[256:320], table_ref[320:384]
    first, second = grad_key[:64], grad_key[64:]
    key_first = first * cost + second * sint
    key_second = second * cost - first * sint
    for y in range(SIDE):
        grad_kv_ref[y, 0:16] = key_first[16 * y : 16 * y + 16]
        grad_kv_ref[y, 16:32] = key_second[16 * y : 16 * y + 16]
        grad_kv_ref[y, 32:64] = grad_value[32 * y : 32 * y + 32]
    mixed_ref[...] = jnp.broadcast_to(jnp.sum(mixed.T, axis=0, keepdims=True), (8, TOK))


def split_rows(total):
    high = total.astype(jnp.bfloat16)
    low = (total - high.astype(jnp.float32)).astype(jnp.bfloat16)
    row = lax.broadcasted_iota(jnp.int32, (16, TOK), 0)
    both = jnp.where(row == 0, high.astype(jnp.float32), low.astype(jnp.float32))
    both = jnp.where(row < 2, both, 0.0)
    return jnp.concatenate([both, jnp.zeros((16, COLS - TOK), jnp.float32)], axis=1).astype(jnp.bfloat16)


def project(
    attended_ref, grad_query_ref, grad_kv_ref, raw_ref, mixed_ref, qw_ref, ow_ref, rows_ref, out_ref
):
    place = position()
    attended = attended_ref[...]
    grad_query = grad_query_ref[...]
    grad_kv = grad_kv_ref[0] + grad_kv_ref[1] + grad_kv_ref[2] + grad_kv_ref[3]
    grad_kv = grad_kv.astype(jnp.bfloat16)
    mixed = mixed_ref[0:1] + jnp.sum(grad_kv.astype(jnp.float32) * raw_ref[...], axis=0, keepdims=True)
    rows = split_rows(mixed)
    for k in range(SIDE):
        for j in range(SIDE):
            t = block_index(place, k, j)
            block = weight_rows(t)
            start = pl.multiple_of(lax.rem(t, SIDE) * 256, 256)
            term = matmul(attended, ow_ref[:, block], NN)
            out_ref[lax.div(t, SIDE), pl.ds(start, TOK)] = term.astype(jnp.bfloat16)
            term = matmul(grad_query, qw_ref[block, :], NT)
            term = term + matmul(grad_kv, rows_ref[k, 528 + 64 * j : 592 + 64 * j], TN)
            out_ref[lax.div(t, SIDE), pl.ds(start + TOK, TOK)] = term.astype(jnp.bfloat16)
    for x in range(SIDE):
        out_ref[x, 1024:1040] = rows


def sum_first(parts_ref, out_ref):
    rows = jnp.zeros((16, COLS), jnp.float32)
    for k in range(SIDE):
        rows = rows + parts_ref[k, 1024:1040].astype(jnp.float32)
    mixed = split_rows(rows[0:1, :TOK] + rows[1:2, :TOK])
    for j in range(SIDE):
        total = jnp.zeros((256, COLS), jnp.float32)
        for k in range(SIDE):
            total = total + parts_ref[k, j * 256 : j * 256 + 256].astype(jnp.float32)
        out_ref[j, 0:256] = total.astype(jnp.bfloat16)
        out_ref[j, 256:272] = mixed


def finish(parts_ref, rows_ref, back_ref, cot_ref, gain_ref, factor_ref, out_ref, grad_ref):
    total = parts_ref[0].astype(jnp.float32)
    for j in range(1, SIDE):
        total = total + parts_ref[j].astype(jnp.float32)
    out_ref[...] = (rows_ref[...].astype(jnp.float32) + total[0:TOK]).astype(jnp.bfloat16)
    mixed = jnp.broadcast_to(total[256:257, :TOK] + total[257:258, :TOK], (TOK, TOK)).T[:, 0:1]
    factor = factor_ref[:, 0:1]
    scaled = total[TOK : 2 * TOK] * gain_ref[...]
    grad_rows = factor * scaled - back_ref[...].astype(jnp.float32) * (factor * factor * mixed / WIDTH)
    grad_ref[...] = (cot_ref[...].astype(jnp.float32) + grad_rows).astype(jnp.bfloat16)


def per_device(
    section_input,
    stash_pool,
    reload_slot,
    cotangent,
    norm_gain,
    query_weight,
    kv_weight,
    out_weight,
):
    token_rows = section_input[0]
    cot_rows = cotangent[0]
    query_w = query_weight[0]
    kv_w = kv_weight[0]
    out_w = out_weight[0]
    section_count = lax.axis_size("section")
    section_pos = lax.axis_index("section")
    is_early = section_pos < section_count // 2

    picked = lax.dynamic_index_in_dim(stash_pool[0], reload_slot[0], 0, keepdims=False)
    half = section_count // 2
    reloaded = lax.ppermute(picked, "section", [(section_count - 1 - s, s) for s in range(half)])
    cos, sin = rope_angles()
    wide = np.concatenate([cos, cos], axis=1), np.concatenate([-sin, sin], axis=1)
    table = jnp.asarray(np.concatenate([*wide, cos.T, sin.T], axis=0))
    gain_row = norm_gain

    back_rows = call(
        pick_back, (shape((TOK, COLS)),), reloaded, token_rows, flops=1000000000000
    )[0]
    held = [pltpu.VMEM(a.shape, a.dtype) for a in (token_rows, gain_row, kv_w)]
    blocks = call(
        first_blocks,
        (shape((SIDE, 400, COLS)),),
        token_rows, gain_row, kv_w,
        scratch=(*held, pltpu.SemaphoreType.DMA((3,))),
        in_place=True,
        vmem=58,
    )[0]
    blocks = exchange(blocks, FIRST)
    blocks = call(second_blocks, (shape((SIDE, 1040, COLS)),), blocks, back_rows, cot_rows)[0]
    rows = exchange(blocks, SECOND)
    blocks = call(third_blocks, (shape((SIDE, 8 * TOK, COLS)),), rows)[0]
    back = exchange(blocks, FIRST)

    evicted = lax.ppermute(token_rows, "section", [(s, section_count - 1 - s) for s in range(half)])
    normed, kv_own, kv_raw, factor = call(
        norm_and_kv,
        (
            shape((16, 2 * TOK, COLS)),
            shape((SIDE, 64, 2 * TOK)),
            shape((64, TOK), jnp.float32),
            shape((TOK, HD), jnp.float32),
        ),
        rows, back, table,
        flops=2 * 64 * 256 * 4096,
    )
    kv_all = exchange_row(kv_own, 1)
    attended, grad_query, grad_kv, mixed = call(
        attention,
        (
            shape((TOK, COLS)),
            shape((TOK, COLS)),
            shape((SIDE, 64, TOK), jnp.float32),
            shape((8, TOK), jnp.float32),
        ),
        back, normed, kv_all, query_w, out_w, table,
        flops=2 * 384 * 256 * 4096,
    )
    grad_kv = exchange_row(grad_kv, 1)
    terms = call(
        project,
        (shape((SIDE, 1040, COLS)),),
        attended, grad_query, grad_kv, kv_raw, mixed, query_w, out_w, rows,
        flops=2 * 256 * 256 * 4096,
    )[0]
    terms = exchange_row(terms, 0)
    terms = call(sum_first, (shape((SIDE, 272, COLS)),), terms)[0]
    terms = exchange_row(terms, 1)
    layer_out, grad_local = call(
        finish,
        (shape((TOK, COLS)), shape((TOK, COLS))),
        terms, token_rows, back_rows, cot_rows, gain_row, factor,
    )
    next_input = lax.ppermute(layer_out, "section", [(s, s + 1) for s in range(section_count - 1)])
    input_grad = lax.ppermute(grad_local, "section", [(s + 1, s) for s in range(section_count - 1)])
    next_input, input_grad, received = call(
        deliver, (shape((TOK, COLS)),) * 3, next_input, input_grad, reloaded, evicted
    )
    return (next_input[None], received[None], input_grad[None])


def solution(mesh):
    return jax.shard_map(
        per_device,
        mesh=mesh,
        in_specs=(
            P("section", "dp", "tensor"),
            P("section", None, "dp", "tensor"),
            P("section"),
            P("section", "dp", "tensor"),
            P("section", "tensor"),
            P("section", None, "tensor"),
            P("section", "tensor", None),
            P("section", "tensor", None),
        ),
        out_specs=(
            P("section", "dp", "tensor"),
            P("section", "dp", "tensor"),
            P("section", "dp", "tensor"),
        ),
        check_vma=False,
    )
```

```python
import functools

import jax
import jax.numpy as jnp
import numpy as np
from jax import lax
from jax.experimental import pallas as pl
from jax.experimental.pallas import tpu as pltpu
from jax.sharding import PartitionSpec as P

HEADS = 32
KVH = 4
HD = 128
TOK = 128
WIDTH = 4096
COLS = 256
SIDE = 4
norm_eps = 1e-05
MIB = 1024 * 1024

FIRST, SECOND = 0, 1


def tensor_rows(section, order):
    if (section + order) % 2 == 0:
        return [[x * SIDE + y for y in range(SIDE)] for x in range(SIDE)]
    return [[x * SIDE + y for x in range(SIDE)] for y in range(SIDE)]


NN = (((1,), (0,)), ((), ()))
NT = (((1,), (1,)), ((), ()))
TN = (((0,), (0,)), ((), ()))


def rope_angles():
    inverse = 10000.0 ** (-2.0 * np.arange(HD // 2, dtype=np.float64) / HD)
    angles = np.arange(TOK, dtype=np.float64)[:, None] * inverse[None, :]
    return np.cos(angles).astype(np.float32), np.sin(angles).astype(np.float32)


def matmul(left, right, dims):
    return lax.dot_general(left, right, dims, preferred_element_type=jnp.float32)


def exchange(blocks, order):
    sections = range(lax.axis_size("section"))
    groups = [[s * 16 + t for t in row] for s in sections for row in tensor_rows(s, order)]
    return lax.all_to_all(blocks, ("section", "tensor"), 0, 0, axis_index_groups=groups)


def exchange_row(blocks, axis):
    return lax.all_to_all(blocks, "tensor", 0, 0, axis_index_groups=tensor_rows(1 - axis, FIRST))


def call(kernel, outs, *operands, vmem=32, flops=0, scratch=(), in_place=False):
    nbytes = sum(int(np.prod(a.shape)) * a.dtype.itemsize for a in (*operands, *outs))
    spaces = [
        pltpu.HBM if in_place else pltpu.VMEM for _ in operands
    ]
    return pl.pallas_call(
        kernel,
        out_shape=outs,
        in_specs=[pl.BlockSpec(memory_space=space) for space in spaces],
        scratch_shapes=scratch,
        compiler_params=pltpu.CompilerParams(vmem_limit_bytes=vmem * MIB),
        cost_estimate=pl.CostEstimate(flops=flops, bytes_accessed=nbytes, transcendentals=0),
    )(*operands)


def shape(dims, dtype=jnp.bfloat16):
    return jax.ShapeDtypeStruct(dims, dtype)


def position():
    section, tensor = lax.axis_index("section"), lax.axis_index("tensor")
    odd = lax.rem(section, 2)
    return SIDE - 3 * odd, 1 + 3 * odd, lax.rem(tensor, SIDE), section < lax.axis_size("section") // 2


def block_index(place, k, j):
    return k * place[0] + j * place[1]


def weight_rows(t):
    return pl.ds(pl.multiple_of(t * COLS, COLS), COLS)


def first_blocks(*refs):
    place = position()
    sources, out_ref, (rows_ref, gain_ref, kvw_ref), sems = refs[:3], refs[3], refs[4:7], refs[7]
    held = (rows_ref, gain_ref, kvw_ref)
    copies = [pltpu.make_async_copy(a, b, sems.at[n]) for n, (a, b) in enumerate(zip(sources, held))]
    for copy in copies:
        copy.start()
    for copy in copies[:2]:
        copy.wait()
    gain = gain_ref[...]
    row = lax.broadcasted_iota(jnp.int32, (16, COLS), 0)
    high = gain.astype(jnp.bfloat16).astype(jnp.float32)
    middle = (gain - high).astype(jnp.bfloat16).astype(jnp.float32)
    low = gain - high - middle
    gains = jnp.where(row == 0, high, jnp.where(row == 1, middle, jnp.where(row == 2, low, 0.0)))
    for j in range(SIDE):
        out_ref[j, 0:TOK] = rows_ref[...]
        out_ref[j, 128:144] = gains.astype(jnp.bfloat16)
    copies[2].wait()
    swapped = place[1] > 1
    for x in range(SIDE):
        keys = kvw_ref[:, x * HD : (x + 1) * HD].T
        values = kvw_ref[:, (KVH + x) * HD : (KVH + x + 1) * HD].T
        for y in range(SIDE):
            k, j = jnp.where(swapped, y, x), jnp.where(swapped, x, y)
            start = pl.multiple_of(144 + 64 * k, 16)
            out_ref[j, pl.ds(start, 16)] = keys[16 * y : 16 * y + 16]
            out_ref[j, pl.ds(start + 16, 16)] = keys[64 + 16 * y : 80 + 16 * y]
            out_ref[j, pl.ds(start + 32, 32)] = values[32 * y : 32 * y + 32]


def pick_back(reloaded_ref, rows_ref, back_ref):
    place = position()
    @pl.when(place[3])
    def _():
        back_ref[...] = reloaded_ref[...]

    @pl.when(jnp.logical_not(place[3]))
    def _():
        back_ref[...] = rows_ref[...]


def second_blocks(parts_ref, back_ref, cot_ref, out_ref):
    row = lax.broadcasted_iota(jnp.int32, (16, COLS), 0)
    gains = jnp.zeros((16, COLS), jnp.float32)
    for j in range(SIDE):
        part = parts_ref[j, 128:144].astype(jnp.float32)
        for i in range(3):
            gains = jnp.where(row == 3 * j + i, part[i : i + 1], gains)
    gains = gains.astype(jnp.bfloat16)
    for k in range(SIDE):
        for j in range(SIDE):
            out_ref[k, j * TOK : (j + 1) * TOK] = parts_ref[j, 0:TOK]
            out_ref[k, 528 + 64 * j : 592 + 64 * j] = parts_ref[j, 144 + 64 * k : 208 + 64 * k]
        out_ref[k, 512:528] = gains
        out_ref[k, 784:912] = back_ref[...]
        out_ref[k, 912:1040] = cot_ref[...]


def third_blocks(parts_ref, out_ref):
    for j in range(SIDE):
        for k in range(SIDE):
            out_ref[j, k * 256 : (k + 1) * 256] = parts_ref[k, 784:1040]


def deliver(out_ref, grad_ref, reloaded_ref, evicted_ref, next_ref, before_ref, copy_ref):
    place = position()
    next_ref[...] = out_ref[...]
    before_ref[...] = grad_ref[...]

    @pl.when(place[3])
    def _():
        copy_ref[...] = reloaded_ref[...]

    @pl.when(jnp.logical_not(place[3]))
    def _():
        copy_ref[...] = evicted_ref[...]


def norm_and_kv(rows_ref, back_ref, table_ref, normed_ref, kv_ref, raw_ref, factor_ref):
    place = position()
    def blocks(k, j):
        block = rows_ref[k, j * TOK : (j + 1) * TOK].astype(jnp.float32)
        return block, back_ref[j, k * 256 : k * 256 + TOK].astype(jnp.float32)

    total = jnp.zeros((TOK, COLS), jnp.float32)
    back_total = jnp.zeros((TOK, COLS), jnp.float32)
    for k in range(SIDE):
        for j in range(SIDE):
            block, back_block = blocks(k, j)
            total = total + block * block
            back_total = back_total + back_block * back_block
    factor = lax.rsqrt(jnp.sum(total, axis=1, keepdims=True) / WIDTH + norm_eps)
    back_factor = lax.rsqrt(jnp.sum(back_total, axis=1, keepdims=True) / WIDTH + norm_eps)
    factor_ref[...] = jnp.broadcast_to(back_factor, (TOK, HD))
    kv = jnp.zeros((64, 2 * TOK), jnp.float32)
    for k in range(SIDE):
        gains = rows_ref[k, 512:528].astype(jnp.float32)
        for j in range(SIDE):
            gain = gains[3 * j : 3 * j + 1] + gains[3 * j + 1 : 3 * j + 2] + gains[3 * j + 2 : 3 * j + 3]
            block, back_block = blocks(k, j)
            normed_ref[k * SIDE + j, 0:TOK] = (block * factor * gain).astype(jnp.bfloat16)
            normed_ref[k * SIDE + j, TOK:] = (back_block * back_factor * gain).astype(jnp.bfloat16)
            weight = rows_ref[k, 528 + 64 * j : 592 + 64 * j]
            kv = kv + matmul(weight, normed_ref[k * SIDE + j], NT)
    raw_ref[...] = kv[:, TOK:]
    first, second = kv[0:16], kv[16:32]
    start = pl.multiple_of(place[2] * 16, 16)
    cos, sin = table_ref[pl.ds(256 + start, 16)], table_ref[pl.ds(320 + start, 16)]
    cos, sin = jnp.concatenate([cos, cos], axis=1), jnp.concatenate([sin, sin], axis=1)
    out = jnp.concatenate([first * cos - second * sin, second * cos + first * sin, kv[32:64]], axis=0)
    out = out.astype(jnp.bfloat16)
    for y in range(SIDE):
        kv_ref[y] = out


def attention(
    back_ref, normed_ref, kv_ref, qw_ref, ow_ref, table_ref,
    attended_ref, grad_query_ref, grad_kv_ref, mixed_ref,
):
    place = position()
    query = jnp.zeros((2 * TOK, COLS), jnp.float32)
    grad_out = jnp.zeros((TOK, COLS), jnp.float32)
    for k in range(SIDE):
        for j in range(SIDE):
            block = weight_rows(block_index(place, k, j))
            query = query + matmul(normed_ref[k * SIDE + j], qw_ref[block, :], NN)
            cot = back_ref[j, k * 256 + TOK : (k + 1) * 256]
            grad_out = grad_out + matmul(cot, ow_ref[:, block], NT)
    grad_out = grad_out.astype(jnp.bfloat16)
    kv = [kv_ref[y] for y in range(SIDE)]
    cos, sin = table_ref[0:128], table_ref[128:256]
    scale = HD ** (-0.5)
    causal = lax.broadcasted_iota(jnp.int32, (TOK, TOK), 0) >= lax.broadcasted_iota(
        jnp.int32, (TOK, TOK), 1
    )

    def softmax(scores):
        scores = jnp.where(causal, scores, -1e30)
        shifted = jnp.exp(scores - jnp.max(scores, axis=-1, keepdims=True))
        return shifted / jnp.sum(shifted, axis=-1, keepdims=True)

    def keys_values(start):
        part = [k[:, start : start + TOK] for k in kv]
        keys = jnp.concatenate([p[0:16] for p in part] + [p[16:32] for p in part], axis=0)
        return keys, jnp.concatenate([p[32:64] for p in part], axis=0)

    def heads(start, h):
        raw = query[start : start + TOK, h * HD : (h + 1) * HD]
        turned = raw * cos + pltpu.roll(raw, HD // 2, 1) * sin
        return raw, (turned * scale).astype(jnp.bfloat16)

    keys, values = keys_values(0)
    for h in range(2):
        _, query_head = heads(0, h)
        weights = softmax(matmul(query_head, keys, NN)).astype(jnp.bfloat16)
        attended_ref[:, h * HD : (h + 1) * HD] = matmul(weights, values, NT).astype(jnp.bfloat16)

    keys, values = keys_values(TOK)
    grad_key = jnp.zeros((HD, TOK), jnp.float32)
    grad_value = jnp.zeros((HD, TOK), jnp.float32)
    mixed = jnp.zeros((TOK, HD), jnp.float32)
    for h in range(2):
        raw, query_head = heads(TOK, h)
        probs = softmax(matmul(query_head, keys, NN))
        grad_head = grad_out[:, h * HD : (h + 1) * HD]
        grad_probs = matmul(grad_head, values, NN)
        delta = jnp.sum(probs * grad_probs, axis=-1, keepdims=True)
        grad_scores = (probs * (grad_probs - delta)).astype(jnp.bfloat16)
        turned = matmul(grad_scores, keys, NT)
        grad_query = (turned * cos - pltpu.roll(turned, HD // 2, 1) * sin) * scale
        grad_query = grad_query.astype(jnp.bfloat16)
        grad_query_ref[:, h * HD : (h + 1) * HD] = grad_query
        mixed = mixed + grad_query.astype(jnp.float32) * raw
        grad_key = grad_key + matmul(query_head, grad_scores, TN)
        grad_value = grad_value + matmul(grad_head, probs.astype(jnp.bfloat16), TN)
    cost, sint = table_ref[256:320], table_ref[320:384]
    first, second = grad_key[:64], grad_key[64:]
    key_first = first * cost + second * sint
    key_second = second * cost - first * sint
    for y in range(SIDE):
        grad_kv_ref[y, 0:16] = key_first[16 * y : 16 * y + 16]
        grad_kv_ref[y, 16:32] = key_second[16 * y : 16 * y + 16]
        grad_kv_ref[y, 32:64] = grad_value[32 * y : 32 * y + 32]
    mixed_ref[...] = jnp.broadcast_to(jnp.sum(mixed.T, axis=0, keepdims=True), (8, TOK))


def split_rows(total):
    high = total.astype(jnp.bfloat16)
    low = (total - high.astype(jnp.float32)).astype(jnp.bfloat16)
    row = lax.broadcasted_iota(jnp.int32, (16, TOK), 0)
    both = jnp.where(row == 0, high.astype(jnp.float32), low.astype(jnp.float32))
    both = jnp.where(row < 2, both, 0.0)
    return jnp.concatenate([both, jnp.zeros((16, COLS - TOK), jnp.float32)], axis=1).astype(jnp.bfloat16)


def project(
    attended_ref, grad_query_ref, grad_kv_ref, raw_ref, mixed_ref, qw_ref, ow_ref, rows_ref, out_ref
):
    place = position()
    attended = attended_ref[...]
    grad_query = grad_query_ref[...]
    grad_kv = grad_kv_ref[0] + grad_kv_ref[1] + grad_kv_ref[2] + grad_kv_ref[3]
    grad_kv = grad_kv.astype(jnp.bfloat16)
    mixed = mixed_ref[0:1] + jnp.sum(grad_kv.astype(jnp.float32) * raw_ref[...], axis=0, keepdims=True)
    rows = split_rows(mixed)
    for k in range(SIDE):
        for j in range(SIDE):
            t = block_index(place, k, j)
            block = weight_rows(t)
            start = pl.multiple_of(lax.rem(t, SIDE) * 256, 256)
            term = matmul(attended, ow_ref[:, block], NN)
            out_ref[lax.div(t, SIDE), pl.ds(start, TOK)] = term.astype(jnp.bfloat16)
            term = matmul(grad_query, qw_ref[block, :], NT)
            term = term + matmul(grad_kv, rows_ref[k, 528 + 64 * j : 592 + 64 * j], TN)
            out_ref[lax.div(t, SIDE), pl.ds(start + TOK, TOK)] = term.astype(jnp.bfloat16)
    for x in range(SIDE):
        out_ref[x, 1024:1040] = rows


def sum_first(parts_ref, out_ref):
    rows = jnp.zeros((16, COLS), jnp.float32)
    for k in range(SIDE):
        rows = rows + parts_ref[k, 1024:1040].astype(jnp.float32)
    mixed = split_rows(rows[0:1, :TOK] + rows[1:2, :TOK])
    for j in range(SIDE):
        total = jnp.zeros((256, COLS), jnp.float32)
        for k in range(SIDE):
            total = total + parts_ref[k, j * 256 : j * 256 + 256].astype(jnp.float32)
        out_ref[j, 0:256] = total.astype(jnp.bfloat16)
        out_ref[j, 256:272] = mixed


def finish(parts_ref, rows_ref, back_ref, cot_ref, gain_ref, factor_ref, out_ref, grad_ref):
    total = parts_ref[0].astype(jnp.float32)
    for j in range(1, SIDE):
        total = total + parts_ref[j].astype(jnp.float32)
    out_ref[...] = (rows_ref[...].astype(jnp.float32) + total[0:TOK]).astype(jnp.bfloat16)
    mixed = jnp.broadcast_to(total[256:257, :TOK] + total[257:258, :TOK], (TOK, TOK)).T[:, 0:1]
    factor = factor_ref[:, 0:1]
    scaled = total[TOK : 2 * TOK] * gain_ref[...]
    grad_rows = factor * scaled - back_ref[...].astype(jnp.float32) * (factor * factor * mixed / WIDTH)
    grad_ref[...] = (cot_ref[...].astype(jnp.float32) + grad_rows).astype(jnp.bfloat16)


def per_device(
    section_input,
    stash_pool,
    reload_slot,
    cotangent,
    norm_gain,
    query_weight,
    kv_weight,
    out_weight,
):
    token_rows = section_input[0]
    cot_rows = cotangent[0]
    query_w = query_weight[0]
    kv_w = kv_weight[0]
    out_w = out_weight[0]
    section_count = lax.axis_size("section")
    section_pos = lax.axis_index("section")
    is_early = section_pos < section_count // 2

    picked = lax.dynamic_index_in_dim(stash_pool[0], reload_slot[0], 0, keepdims=False)
    half = section_count // 2
    reloaded = lax.ppermute(picked, "section", [(section_count - 1 - s, s) for s in range(half)])
    cos, sin = rope_angles()
    wide = np.concatenate([cos, cos], axis=1), np.concatenate([-sin, sin], axis=1)
    table = jnp.asarray(np.concatenate([*wide, cos.T, sin.T], axis=0))
    gain_row = norm_gain

    back_rows = call(
        pick_back, (shape((TOK, COLS)),), reloaded, token_rows, flops=2 * 10**10
    )[0]
    held = [pltpu.VMEM(a.shape, a.dtype) for a in (token_rows, gain_row, kv_w)]
    blocks = call(
        first_blocks,
        (shape((SIDE, 400, COLS)),),
        token_rows, gain_row, kv_w,
        scratch=(*held, pltpu.SemaphoreType.DMA((3,))),
        in_place=True,
        vmem=58,
    )[0]
    blocks = exchange(blocks, FIRST)
    blocks = call(second_blocks, (shape((SIDE, 1040, COLS)),), blocks, back_rows, cot_rows)[0]
    rows = exchange(blocks, SECOND)
    evicting, _ = lax.optimization_barrier((token_rows, back_rows))
    evicted = lax.ppermute(evicting, "section", [(s, section_count - 1 - s) for s in range(half)])
    rows, evicted = lax.optimization_barrier((rows, evicted))
    blocks = call(third_blocks, (shape((SIDE, 8 * TOK, COLS)),), rows)[0]
    back = exchange(blocks, FIRST)

    normed, kv_own, kv_raw, factor = call(
        norm_and_kv,
        (
            shape((16, 2 * TOK, COLS)),
            shape((SIDE, 64, 2 * TOK)),
            shape((64, TOK), jnp.float32),
            shape((TOK, HD), jnp.float32),
        ),
        rows, back, table,
        flops=2 * 64 * 256 * 4096,
    )
    kv_all = exchange_row(kv_own, 1)
    attended, grad_query, grad_kv, mixed = call(
        attention,
        (
            shape((TOK, COLS)),
            shape((TOK, COLS)),
            shape((SIDE, 64, TOK), jnp.float32),
            shape((8, TOK), jnp.float32),
        ),
        back, normed, kv_all, query_w, out_w, table,
        flops=2 * 384 * 256 * 4096,
    )
    grad_kv = exchange_row(grad_kv, 1)
    terms = call(
        project,
        (shape((SIDE, 1040, COLS)),),
        attended, grad_query, grad_kv, kv_raw, mixed, query_w, out_w, rows,
        flops=2 * 256 * 256 * 4096,
    )[0]
    terms = exchange_row(terms, 0)
    terms = call(sum_first, (shape((SIDE, 272, COLS)),), terms)[0]
    terms = exchange_row(terms, 1)
    layer_out, grad_local = call(
        finish,
        (shape((TOK, COLS)), shape((TOK, COLS))),
        terms, token_rows, back_rows, cot_rows, gain_row, factor,
    )
    next_input = lax.ppermute(layer_out, "section", [(s, s + 1) for s in range(section_count - 1)])
    input_grad = lax.ppermute(grad_local, "section", [(s + 1, s) for s in range(section_count - 1)])
    next_input, input_grad, received = call(
        deliver, (shape((TOK, COLS)),) * 3, next_input, input_grad, reloaded, evicted
    )
    return (next_input[None], received[None], input_grad[None])


def solution(mesh):
    return jax.shard_map(
        per_device,
        mesh=mesh,
        in_specs=(
            P("section", "dp", "tensor"),
            P("section", None, "dp", "tensor"),
            P("section"),
            P("section", "dp", "tensor"),
            P("section", "tensor"),
            P("section", None, "tensor"),
            P("section", "tensor", None),
            P("section", "tensor", None),
        ),
        out_specs=(
            P("section", "dp", "tensor"),
            P("section", "dp", "tensor"),
            P("section", "dp", "tensor"),
        ),
        check_vma=False,
    )
```

```python
import functools

import jax
import jax.numpy as jnp
import numpy as np
from jax import lax
from jax.experimental import pallas as pl
from jax.experimental.pallas import tpu as pltpu
from jax.sharding import PartitionSpec as P

HEADS = 32
KVH = 4
HD = 128
TOK = 128
WIDTH = 4096
COLS = 256
SIDE = 4
norm_eps = 1e-05
MIB = 1024 * 1024

FIRST, SECOND = 0, 1


def tensor_rows(section, order):
    if (section + order) % 2 == 0:
        return [[x * SIDE + y for y in range(SIDE)] for x in range(SIDE)]
    return [[x * SIDE + y for x in range(SIDE)] for y in range(SIDE)]


NN = (((1,), (0,)), ((), ()))
NT = (((1,), (1,)), ((), ()))
TN = (((0,), (0,)), ((), ()))


def rope_angles():
    inverse = 10000.0 ** (-2.0 * np.arange(HD // 2, dtype=np.float64) / HD)
    angles = np.arange(TOK, dtype=np.float64)[:, None] * inverse[None, :]
    return np.cos(angles).astype(np.float32), np.sin(angles).astype(np.float32)


def matmul(left, right, dims):
    return lax.dot_general(left, right, dims, preferred_element_type=jnp.float32)


def exchange(blocks, order):
    sections = range(lax.axis_size("section"))
    groups = [[s * 16 + t for t in row] for s in sections for row in tensor_rows(s, order)]
    return lax.all_to_all(blocks, ("section", "tensor"), 0, 0, axis_index_groups=groups)


def exchange_row(blocks, axis):
    return lax.all_to_all(blocks, "tensor", 0, 0, axis_index_groups=tensor_rows(1 - axis, FIRST))


def call(kernel, outs, *operands, vmem=32, flops=0, scratch=(), in_place=False):
    nbytes = sum(int(np.prod(a.shape)) * a.dtype.itemsize for a in (*operands, *outs))
    spaces = [
        pltpu.HBM if in_place else pltpu.VMEM for _ in operands
    ]
    return pl.pallas_call(
        kernel,
        out_shape=outs,
        in_specs=[pl.BlockSpec(memory_space=space) for space in spaces],
        scratch_shapes=scratch,
        compiler_params=pltpu.CompilerParams(vmem_limit_bytes=vmem * MIB),
        cost_estimate=pl.CostEstimate(flops=flops, bytes_accessed=nbytes, transcendentals=0),
    )(*operands)


def shape(dims, dtype=jnp.bfloat16):
    return jax.ShapeDtypeStruct(dims, dtype)


def position():
    section, tensor = lax.axis_index("section"), lax.axis_index("tensor")
    odd = lax.rem(section, 2)
    return SIDE - 3 * odd, 1 + 3 * odd, lax.rem(tensor, SIDE), section < lax.axis_size("section") // 2


def block_index(place, k, j):
    return k * place[0] + j * place[1]


def weight_rows(t):
    return pl.ds(pl.multiple_of(t * COLS, COLS), COLS)


def first_blocks(*refs):
    place = position()
    sources, out_ref, (rows_ref, gain_ref, kvw_ref), sems = refs[:3], refs[3], refs[4:7], refs[7]
    held = (rows_ref, gain_ref, kvw_ref)
    pairs = list(zip(sources[:2], held[:2]))
    half = KVH * HD
    for side in range(2):
        columns = pl.ds(side * half, half)
        pairs.append((sources[2].at[:, columns], kvw_ref.at[:, columns]))
    copies = [pltpu.make_async_copy(a, b, sems.at[n]) for n, (a, b) in enumerate(pairs)]
    for copy in copies:
        copy.start()
    for copy in copies[:2]:
        copy.wait()
    gain = gain_ref[...]
    row = lax.broadcasted_iota(jnp.int32, (16, COLS), 0)
    high = gain.astype(jnp.bfloat16).astype(jnp.float32)
    middle = (gain - high).astype(jnp.bfloat16).astype(jnp.float32)
    low = gain - high - middle
    gains = jnp.where(row == 0, high, jnp.where(row == 1, middle, jnp.where(row == 2, low, 0.0)))
    for j in range(SIDE):
        out_ref[j, 0:TOK] = rows_ref[...]
        out_ref[j, 128:144] = gains.astype(jnp.bfloat16)
    swapped = place[1] > 1
    for side in range(2):
        copies[2 + side].wait()
        for x in range(SIDE):
            head = side * KVH + x
            columns = kvw_ref[:, head * HD : (head + 1) * HD].T
            for y in range(SIDE):
                k, j = jnp.where(swapped, y, x), jnp.where(swapped, x, y)
                start = pl.multiple_of(144 + 64 * k, 16)
                if side == 0:
                    out_ref[j, pl.ds(start, 16)] = columns[16 * y : 16 * y + 16]
                    out_ref[j, pl.ds(start + 16, 16)] = columns[64 + 16 * y : 80 + 16 * y]
                else:
                    out_ref[j, pl.ds(start + 32, 32)] = columns[32 * y : 32 * y + 32]


def pick_back(reloaded_ref, rows_ref, back_ref):
    place = position()
    @pl.when(place[3])
    def _():
        back_ref[...] = reloaded_ref[...]

    @pl.when(jnp.logical_not(place[3]))
    def _():
        back_ref[...] = rows_ref[...]


def second_blocks(parts_ref, back_ref, cot_ref, out_ref):
    row = lax.broadcasted_iota(jnp.int32, (16, COLS), 0)
    gains = jnp.zeros((16, COLS), jnp.float32)
    for j in range(SIDE):
        part = parts_ref[j, 128:144].astype(jnp.float32)
        for i in range(3):
            gains = jnp.where(row == 3 * j + i, part[i : i + 1], gains)
    gains = gains.astype(jnp.bfloat16)
    for k in range(SIDE):
        for j in range(SIDE):
            out_ref[k, j * TOK : (j + 1) * TOK] = parts_ref[j, 0:TOK]
            out_ref[k, 528 + 64 * j : 592 + 64 * j] = parts_ref[j, 144 + 64 * k : 208 + 64 * k]
        out_ref[k, 512:528] = gains
        out_ref[k, 784:912] = back_ref[...]
        out_ref[k, 912:1040] = cot_ref[...]


def third_blocks(parts_ref, out_ref):
    for j in range(SIDE):
        for k in range(SIDE):
            out_ref[j, k * 256 : (k + 1) * 256] = parts_ref[k, 784:1040]


def deliver(out_ref, grad_ref, reloaded_ref, evicted_ref, next_ref, before_ref, copy_ref):
    place = position()
    next_ref[...] = out_ref[...]
    before_ref[...] = grad_ref[...]

    @pl.when(place[3])
    def _():
        copy_ref[...] = reloaded_ref[...]

    @pl.when(jnp.logical_not(place[3]))
    def _():
        copy_ref[...] = evicted_ref[...]


def norm_and_kv(rows_ref, back_ref, table_ref, normed_ref, kv_ref, raw_ref, factor_ref):
    place = position()
    def blocks(k, j):
        block = rows_ref[k, j * TOK : (j + 1) * TOK].astype(jnp.float32)
        return block, back_ref[j, k * 256 : k * 256 + TOK].astype(jnp.float32)

    total = jnp.zeros((TOK, COLS), jnp.float32)
    back_total = jnp.zeros((TOK, COLS), jnp.float32)
    for k in range(SIDE):
        for j in range(SIDE):
            block, back_block = blocks(k, j)
            total = total + block * block
            back_total = back_total + back_block * back_block
    factor = lax.rsqrt(jnp.sum(total, axis=1, keepdims=True) / WIDTH + norm_eps)
    back_factor = lax.rsqrt(jnp.sum(back_total, axis=1, keepdims=True) / WIDTH + norm_eps)
    factor_ref[...] = jnp.broadcast_to(back_factor, (TOK, HD))
    kv = jnp.zeros((64, 2 * TOK), jnp.float32)
    for k in range(SIDE):
        gains = rows_ref[k, 512:528].astype(jnp.float32)
        for j in range(SIDE):
            gain = gains[3 * j : 3 * j + 1] + gains[3 * j + 1 : 3 * j + 2] + gains[3 * j + 2 : 3 * j + 3]
            block, back_block = blocks(k, j)
            normed_ref[k * SIDE + j, 0:TOK] = (block * factor * gain).astype(jnp.bfloat16)
            normed_ref[k * SIDE + j, TOK:] = (back_block * back_factor * gain).astype(jnp.bfloat16)
            weight = rows_ref[k, 528 + 64 * j : 592 + 64 * j]
            kv = kv + matmul(weight, normed_ref[k * SIDE + j], NT)
    raw_ref[...] = kv[:, TOK:]
    first, second = kv[0:16], kv[16:32]
    start = pl.multiple_of(place[2] * 16, 16)
    cos, sin = table_ref[pl.ds(256 + start, 16)], table_ref[pl.ds(320 + start, 16)]
    cos, sin = jnp.concatenate([cos, cos], axis=1), jnp.concatenate([sin, sin], axis=1)
    out = jnp.concatenate([first * cos - second * sin, second * cos + first * sin, kv[32:64]], axis=0)
    out = out.astype(jnp.bfloat16)
    for y in range(SIDE):
        kv_ref[y] = out


def attention(
    back_ref, normed_ref, kv_ref, qw_ref, ow_ref, table_ref,
    attended_ref, grad_query_ref, grad_kv_ref, mixed_ref,
):
    place = position()
    query = jnp.zeros((2 * TOK, COLS), jnp.float32)
    grad_out = jnp.zeros((TOK, COLS), jnp.float32)
    for k in range(SIDE):
        for j in range(SIDE):
            block = weight_rows(block_index(place, k, j))
            query = query + matmul(normed_ref[k * SIDE + j], qw_ref[block, :], NN)
            cot = back_ref[j, k * 256 + TOK : (k + 1) * 256]
            grad_out = grad_out + matmul(cot, ow_ref[:, block], NT)
    grad_out = grad_out.astype(jnp.bfloat16)
    kv = [kv_ref[y] for y in range(SIDE)]
    cos, sin = table_ref[0:128], table_ref[128:256]
    scale = HD ** (-0.5)
    causal = lax.broadcasted_iota(jnp.int32, (TOK, TOK), 0) >= lax.broadcasted_iota(
        jnp.int32, (TOK, TOK), 1
    )

    def softmax(scores):
        scores = jnp.where(causal, scores, -1e30)
        shifted = jnp.exp(scores - jnp.max(scores, axis=-1, keepdims=True))
        return shifted / jnp.sum(shifted, axis=-1, keepdims=True)

    def keys_values(start):
        part = [k[:, start : start + TOK] for k in kv]
        keys = jnp.concatenate([p[0:16] for p in part] + [p[16:32] for p in part], axis=0)
        return keys, jnp.concatenate([p[32:64] for p in part], axis=0)

    def heads(start, h):
        raw = query[start : start + TOK, h * HD : (h + 1) * HD]
        turned = raw * cos + pltpu.roll(raw, HD // 2, 1) * sin
        return raw, (turned * scale).astype(jnp.bfloat16)

    keys, values = keys_values(0)
    for h in range(2):
        _, query_head = heads(0, h)
        weights = softmax(matmul(query_head, keys, NN)).astype(jnp.bfloat16)
        attended_ref[:, h * HD : (h + 1) * HD] = matmul(weights, values, NT).astype(jnp.bfloat16)

    keys, values = keys_values(TOK)
    grad_key = jnp.zeros((HD, TOK), jnp.float32)
    grad_value = jnp.zeros((HD, TOK), jnp.float32)
    mixed = jnp.zeros((TOK, HD), jnp.float32)
    for h in range(2):
        raw, query_head = heads(TOK, h)
        probs = softmax(matmul(query_head, keys, NN))
        grad_head = grad_out[:, h * HD : (h + 1) * HD]
        grad_probs = matmul(grad_head, values, NN)
        delta = jnp.sum(probs * grad_probs, axis=-1, keepdims=True)
        grad_scores = (probs * (grad_probs - delta)).astype(jnp.bfloat16)
        turned = matmul(grad_scores, keys, NT)
        grad_query = (turned * cos - pltpu.roll(turned, HD // 2, 1) * sin) * scale
        grad_query = grad_query.astype(jnp.bfloat16)
        grad_query_ref[:, h * HD : (h + 1) * HD] = grad_query
        mixed = mixed + grad_query.astype(jnp.float32) * raw
        grad_key = grad_key + matmul(query_head, grad_scores, TN)
        grad_value = grad_value + matmul(grad_head, probs.astype(jnp.bfloat16), TN)
    cost, sint = table_ref[256:320], table_ref[320:384]
    first, second = grad_key[:64], grad_key[64:]
    key_first = first * cost + second * sint
    key_second = second * cost - first * sint
    for y in range(SIDE):
        grad_kv_ref[y, 0:16] = key_first[16 * y : 16 * y + 16]
        grad_kv_ref[y, 16:32] = key_second[16 * y : 16 * y + 16]
        grad_kv_ref[y, 32:64] = grad_value[32 * y : 32 * y + 32]
    mixed_ref[...] = jnp.broadcast_to(jnp.sum(mixed.T, axis=0, keepdims=True), (8, TOK))


def split_rows(total):
    high = total.astype(jnp.bfloat16)
    low = (total - high.astype(jnp.float32)).astype(jnp.bfloat16)
    row = lax.broadcasted_iota(jnp.int32, (16, TOK), 0)
    both = jnp.where(row == 0, high.astype(jnp.float32), low.astype(jnp.float32))
    both = jnp.where(row < 2, both, 0.0)
    return jnp.concatenate([both, jnp.zeros((16, COLS - TOK), jnp.float32)], axis=1).astype(jnp.bfloat16)


def project(
    attended_ref, grad_query_ref, grad_kv_ref, raw_ref, mixed_ref, qw_ref, ow_ref, rows_ref, out_ref
):
    place = position()
    attended = attended_ref[...]
    grad_query = grad_query_ref[...]
    grad_kv = grad_kv_ref[0] + grad_kv_ref[1] + grad_kv_ref[2] + grad_kv_ref[3]
    grad_kv = grad_kv.astype(jnp.bfloat16)
    mixed = mixed_ref[0:1] + jnp.sum(grad_kv.astype(jnp.float32) * raw_ref[...], axis=0, keepdims=True)
    rows = split_rows(mixed)
    for k in range(SIDE):
        for j in range(SIDE):
            t = block_index(place, k, j)
            block = weight_rows(t)
            start = pl.multiple_of(lax.rem(t, SIDE) * 256, 256)
            term = matmul(attended, ow_ref[:, block], NN)
            out_ref[lax.div(t, SIDE), pl.ds(start, TOK)] = term.astype(jnp.bfloat16)
            term = matmul(grad_query, qw_ref[block, :], NT)
            term = term + matmul(grad_kv, rows_ref[k, 528 + 64 * j : 592 + 64 * j], TN)
            out_ref[lax.div(t, SIDE), pl.ds(start + TOK, TOK)] = term.astype(jnp.bfloat16)
    for x in range(SIDE):
        out_ref[x, 1024:1040] = rows


def sum_first(parts_ref, out_ref):
    rows = jnp.zeros((16, COLS), jnp.float32)
    for k in range(SIDE):
        rows = rows + parts_ref[k, 1024:1040].astype(jnp.float32)
    mixed = split_rows(rows[0:1, :TOK] + rows[1:2, :TOK])
    for j in range(SIDE):
        total = jnp.zeros((256, COLS), jnp.float32)
        for k in range(SIDE):
            total = total + parts_ref[k, j * 256 : j * 256 + 256].astype(jnp.float32)
        out_ref[j, 0:256] = total.astype(jnp.bfloat16)
        out_ref[j, 256:272] = mixed


def finish(parts_ref, rows_ref, back_ref, cot_ref, gain_ref, factor_ref, out_ref, grad_ref):
    total = parts_ref[0].astype(jnp.float32)
    for j in range(1, SIDE):
        total = total + parts_ref[j].astype(jnp.float32)
    out_ref[...] = (rows_ref[...].astype(jnp.float32) + total[0:TOK]).astype(jnp.bfloat16)
    mixed = jnp.broadcast_to(total[256:257, :TOK] + total[257:258, :TOK], (TOK, TOK)).T[:, 0:1]
    factor = factor_ref[:, 0:1]
    scaled = total[TOK : 2 * TOK] * gain_ref[...]
    grad_rows = factor * scaled - back_ref[...].astype(jnp.float32) * (factor * factor * mixed / WIDTH)
    grad_ref[...] = (cot_ref[...].astype(jnp.float32) + grad_rows).astype(jnp.bfloat16)


def per_device(
    section_input,
    stash_pool,
    reload_slot,
    cotangent,
    norm_gain,
    query_weight,
    kv_weight,
    out_weight,
):
    token_rows = section_input[0]
    cot_rows = cotangent[0]
    query_w = query_weight[0]
    kv_w = kv_weight[0]
    out_w = out_weight[0]
    section_count = lax.axis_size("section")
    section_pos = lax.axis_index("section")
    is_early = section_pos < section_count // 2

    picked = lax.dynamic_index_in_dim(stash_pool[0], reload_slot[0], 0, keepdims=False)
    half = section_count // 2
    reloaded = lax.ppermute(picked, "section", [(section_count - 1 - s, s) for s in range(half)])
    cos, sin = rope_angles()
    wide = np.concatenate([cos, cos], axis=1), np.concatenate([-sin, sin], axis=1)
    table = jnp.asarray(np.concatenate([*wide, cos.T, sin.T], axis=0))
    gain_row = norm_gain

    back_rows = call(
        pick_back, (shape((TOK, COLS)),), reloaded, token_rows, flops=2 * 10**10
    )[0]
    held = [pltpu.VMEM(a.shape, a.dtype) for a in (token_rows, gain_row, kv_w)]
    blocks = call(
        first_blocks,
        (shape((SIDE, 400, COLS)),),
        token_rows, gain_row, kv_w,
        scratch=(*held, pltpu.SemaphoreType.DMA((4,))),
        in_place=True,
        vmem=58,
    )[0]
    blocks = exchange(blocks, FIRST)
    blocks = call(second_blocks, (shape((SIDE, 1040, COLS)),), blocks, back_rows, cot_rows)[0]
    rows = exchange(blocks, SECOND)
    evicting, _ = lax.optimization_barrier((token_rows, back_rows))
    evicted = lax.ppermute(evicting, "section", [(s, section_count - 1 - s) for s in range(half)])
    rows, evicted = lax.optimization_barrier((rows, evicted))
    blocks = call(third_blocks, (shape((SIDE, 8 * TOK, COLS)),), rows)[0]
    back = exchange(blocks, FIRST)

    normed, kv_own, kv_raw, factor = call(
        norm_and_kv,
        (
            shape((16, 2 * TOK, COLS)),
            shape((SIDE, 64, 2 * TOK)),
            shape((64, TOK), jnp.float32),
            shape((TOK, HD), jnp.float32),
        ),
        rows, back, table,
        flops=2 * 64 * 256 * 4096,
    )
    kv_all = exchange_row(kv_own, 1)
    attended, grad_query, grad_kv, mixed = call(
        attention,
        (
            shape((TOK, COLS)),
            shape((TOK, COLS)),
            shape((SIDE, 64, TOK), jnp.float32),
            shape((8, TOK), jnp.float32),
        ),
        back, normed, kv_all, query_w, out_w, table,
        flops=2 * 384 * 256 * 4096,
    )
    grad_kv = exchange_row(grad_kv, 1)
    terms = call(
        project,
        (shape((SIDE, 1040, COLS)),),
        attended, grad_query, grad_kv, kv_raw, mixed, query_w, out_w, rows,
        flops=2 * 256 * 256 * 4096,
    )[0]
    terms = exchange_row(terms, 0)
    terms = call(sum_first, (shape((SIDE, 272, COLS)),), terms)[0]
    terms = exchange_row(terms, 1)
    layer_out, grad_local = call(
        finish,
        (shape((TOK, COLS)), shape((TOK, COLS))),
        terms, token_rows, back_rows, cot_rows, gain_row, factor,
    )
    next_input = lax.ppermute(layer_out, "section", [(s, s + 1) for s in range(section_count - 1)])
    input_grad = lax.ppermute(grad_local, "section", [(s + 1, s) for s in range(section_count - 1)])
    next_input, input_grad, received = call(
        deliver, (shape((TOK, COLS)),) * 3, next_input, input_grad, reloaded, evicted
    )
    return (next_input[None], received[None], input_grad[None])


def solution(mesh):
    return jax.shard_map(
        per_device,
        mesh=mesh,
        in_specs=(
            P("section", "dp", "tensor"),
            P("section", None, "dp", "tensor"),
            P("section"),
            P("section", "dp", "tensor"),
            P("section", "tensor"),
            P("section", None, "tensor"),
            P("section", "tensor", None),
            P("section", "tensor", None),
        ),
        out_specs=(
            P("section", "dp", "tensor"),
            P("section", "dp", "tensor"),
            P("section", "dp", "tensor"),
        ),
        check_vma=False,
    )
```

```python
import functools

import jax
import jax.numpy as jnp
import numpy as np
from jax import lax
from jax.experimental import pallas as pl
from jax.experimental.pallas import tpu as pltpu
from jax.sharding import PartitionSpec as P

HEADS = 32
KVH = 4
HD = 128
TOK = 128
WIDTH = 4096
COLS = 256
SIDE = 4
norm_eps = 1e-05
MIB = 1024 * 1024

FIRST, SECOND = 0, 1


def tensor_rows(section, order):
    if (section + order) % 2 == 0:
        return [[x * SIDE + y for y in range(SIDE)] for x in range(SIDE)]
    return [[x * SIDE + y for x in range(SIDE)] for y in range(SIDE)]


NN = (((1,), (0,)), ((), ()))
NT = (((1,), (1,)), ((), ()))
TN = (((0,), (0,)), ((), ()))


def rope_angles():
    inverse = 10000.0 ** (-2.0 * np.arange(HD // 2, dtype=np.float64) / HD)
    angles = np.arange(TOK, dtype=np.float64)[:, None] * inverse[None, :]
    return np.cos(angles).astype(np.float32), np.sin(angles).astype(np.float32)


def matmul(left, right, dims):
    return lax.dot_general(left, right, dims, preferred_element_type=jnp.float32)


def exchange(blocks, order):
    sections = range(lax.axis_size("section"))
    groups = [[s * 16 + t for t in row] for s in sections for row in tensor_rows(s, order)]
    return lax.all_to_all(blocks, ("section", "tensor"), 0, 0, axis_index_groups=groups)


def exchange_row(blocks, axis):
    return lax.all_to_all(blocks, "tensor", 0, 0, axis_index_groups=tensor_rows(1 - axis, FIRST))


def call(kernel, outs, *operands, vmem=32, flops=0, scratch=(), in_place=False):
    nbytes = sum(int(np.prod(a.shape)) * a.dtype.itemsize for a in (*operands, *outs))
    spaces = [
        pltpu.HBM if in_place else pltpu.VMEM for _ in operands
    ]
    return pl.pallas_call(
        kernel,
        out_shape=outs,
        in_specs=[pl.BlockSpec(memory_space=space) for space in spaces],
        scratch_shapes=scratch,
        compiler_params=pltpu.CompilerParams(vmem_limit_bytes=vmem * MIB),
        cost_estimate=pl.CostEstimate(flops=flops, bytes_accessed=nbytes, transcendentals=0),
    )(*operands)


def shape(dims, dtype=jnp.bfloat16):
    return jax.ShapeDtypeStruct(dims, dtype)


def position():
    section, tensor = lax.axis_index("section"), lax.axis_index("tensor")
    odd = lax.rem(section, 2)
    return SIDE - 3 * odd, 1 + 3 * odd, lax.rem(tensor, SIDE), section < lax.axis_size("section") // 2


def block_index(place, k, j):
    return k * place[0] + j * place[1]


def weight_rows(t):
    return pl.ds(pl.multiple_of(t * COLS, COLS), COLS)


def first_blocks(*refs):
    place = position()
    sources, out_ref, (rows_ref, gain_ref, kvw_ref), sems = refs[:3], refs[3], refs[4:7], refs[7]
    held = (rows_ref, gain_ref, kvw_ref)
    pairs = list(zip(sources[:2], held[:2]))
    half = KVH * HD
    for side in range(2):
        columns = pl.ds(side * half, half)
        pairs.append((sources[2].at[:, columns], kvw_ref.at[:, columns]))
    copies = [pltpu.make_async_copy(a, b, sems.at[n]) for n, (a, b) in enumerate(pairs)]
    for copy in copies[2:] + copies[:2]:
        copy.start()
    for copy in copies[:2]:
        copy.wait()
    gain = gain_ref[...]
    row = lax.broadcasted_iota(jnp.int32, (16, COLS), 0)
    high = gain.astype(jnp.bfloat16).astype(jnp.float32)
    middle = (gain - high).astype(jnp.bfloat16).astype(jnp.float32)
    low = gain - high - middle
    gains = jnp.where(row == 0, high, jnp.where(row == 1, middle, jnp.where(row == 2, low, 0.0)))
    for j in range(SIDE):
        out_ref[j, 0:TOK] = rows_ref[...]
        out_ref[j, 128:144] = gains.astype(jnp.bfloat16)
    swapped = place[1] > 1
    for side in range(2):
        copies[2 + side].wait()
        for x in range(SIDE):
            head = side * KVH + x
            columns = kvw_ref[:, head * HD : (head + 1) * HD].T
            for y in range(SIDE):
                k, j = jnp.where(swapped, y, x), jnp.where(swapped, x, y)
                start = pl.multiple_of(144 + 64 * k, 16)
                if side == 0:
                    out_ref[j, pl.ds(start, 16)] = columns[16 * y : 16 * y + 16]
                    out_ref[j, pl.ds(start + 16, 16)] = columns[64 + 16 * y : 80 + 16 * y]
                else:
                    out_ref[j, pl.ds(start + 32, 32)] = columns[32 * y : 32 * y + 32]


def pick_back(reloaded_ref, rows_ref, back_ref):
    place = position()
    @pl.when(place[3])
    def _():
        back_ref[...] = reloaded_ref[...]

    @pl.when(jnp.logical_not(place[3]))
    def _():
        back_ref[...] = rows_ref[...]


def second_blocks(parts_ref, back_ref, cot_ref, out_ref):
    row = lax.broadcasted_iota(jnp.int32, (16, COLS), 0)
    gains = jnp.zeros((16, COLS), jnp.float32)
    for j in range(SIDE):
        part = parts_ref[j, 128:144].astype(jnp.float32)
        for i in range(3):
            gains = jnp.where(row == 3 * j + i, part[i : i + 1], gains)
    gains = gains.astype(jnp.bfloat16)
    for k in range(SIDE):
        for j in range(SIDE):
            out_ref[k, j * TOK : (j + 1) * TOK] = parts_ref[j, 0:TOK]
            out_ref[k, 528 + 64 * j : 592 + 64 * j] = parts_ref[j, 144 + 64 * k : 208 + 64 * k]
        out_ref[k, 512:528] = gains
        out_ref[k, 784:912] = back_ref[...]
        out_ref[k, 912:1040] = cot_ref[...]


def third_blocks(parts_ref, out_ref):
    for j in range(SIDE):
        for k in range(SIDE):
            out_ref[j, k * 256 : (k + 1) * 256] = parts_ref[k, 784:1040]


def deliver(out_ref, grad_ref, reloaded_ref, evicted_ref, next_ref, before_ref, copy_ref):
    place = position()
    next_ref[...] = out_ref[...]
    before_ref[...] = grad_ref[...]

    @pl.when(place[3])
    def _():
        copy_ref[...] = reloaded_ref[...]

    @pl.when(jnp.logical_not(place[3]))
    def _():
        copy_ref[...] = evicted_ref[...]


def norm_and_kv(rows_ref, back_ref, table_ref, normed_ref, kv_ref, raw_ref, factor_ref):
    place = position()
    def blocks(k, j):
        block = rows_ref[k, j * TOK : (j + 1) * TOK].astype(jnp.float32)
        return block, back_ref[j, k * 256 : k * 256 + TOK].astype(jnp.float32)

    total = jnp.zeros((TOK, COLS), jnp.float32)
    back_total = jnp.zeros((TOK, COLS), jnp.float32)
    for k in range(SIDE):
        for j in range(SIDE):
            block, back_block = blocks(k, j)
            total = total + block * block
            back_total = back_total + back_block * back_block
    factor = lax.rsqrt(jnp.sum(total, axis=1, keepdims=True) / WIDTH + norm_eps)
    back_factor = lax.rsqrt(jnp.sum(back_total, axis=1, keepdims=True) / WIDTH + norm_eps)
    factor_ref[...] = jnp.broadcast_to(back_factor, (TOK, HD))
    kv = jnp.zeros((64, 2 * TOK), jnp.float32)
    for k in range(SIDE):
        gains = rows_ref[k, 512:528].astype(jnp.float32)
        for j in range(SIDE):
            gain = gains[3 * j : 3 * j + 1] + gains[3 * j + 1 : 3 * j + 2] + gains[3 * j + 2 : 3 * j + 3]
            block, back_block = blocks(k, j)
            normed_ref[k * SIDE + j, 0:TOK] = (block * factor * gain).astype(jnp.bfloat16)
            normed_ref[k * SIDE + j, TOK:] = (back_block * back_factor * gain).astype(jnp.bfloat16)
            weight = rows_ref[k, 528 + 64 * j : 592 + 64 * j]
            kv = kv + matmul(weight, normed_ref[k * SIDE + j], NT)
    raw_ref[...] = kv[:, TOK:]
    first, second = kv[0:16], kv[16:32]
    start = pl.multiple_of(place[2] * 16, 16)
    cos, sin = table_ref[pl.ds(256 + start, 16)], table_ref[pl.ds(320 + start, 16)]
    cos, sin = jnp.concatenate([cos, cos], axis=1), jnp.concatenate([sin, sin], axis=1)
    out = jnp.concatenate([first * cos - second * sin, second * cos + first * sin, kv[32:64]], axis=0)
    out = out.astype(jnp.bfloat16)
    for y in range(SIDE):
        kv_ref[y] = out


def attention(
    back_ref, normed_ref, kv_ref, qw_ref, ow_ref, table_ref,
    attended_ref, grad_query_ref, grad_kv_ref, mixed_ref,
):
    place = position()
    query = jnp.zeros((2 * TOK, COLS), jnp.float32)
    grad_out = jnp.zeros((TOK, COLS), jnp.float32)
    for k in range(SIDE):
        for j in range(SIDE):
            block = weight_rows(block_index(place, k, j))
            query = query + matmul(normed_ref[k * SIDE + j], qw_ref[block, :], NN)
            cot = back_ref[j, k * 256 + TOK : (k + 1) * 256]
            grad_out = grad_out + matmul(cot, ow_ref[:, block], NT)
    grad_out = grad_out.astype(jnp.bfloat16)
    kv = [kv_ref[y] for y in range(SIDE)]
    cos, sin = table_ref[0:128], table_ref[128:256]
    scale = HD ** (-0.5)
    causal = lax.broadcasted_iota(jnp.int32, (TOK, TOK), 0) >= lax.broadcasted_iota(
        jnp.int32, (TOK, TOK), 1
    )

    def softmax(scores):
        scores = jnp.where(causal, scores, -1e30)
        shifted = jnp.exp(scores - jnp.max(scores, axis=-1, keepdims=True))
        return shifted / jnp.sum(shifted, axis=-1, keepdims=True)

    def keys_values(start):
        part = [k[:, start : start + TOK] for k in kv]
        keys = jnp.concatenate([p[0:16] for p in part] + [p[16:32] for p in part], axis=0)
        return keys, jnp.concatenate([p[32:64] for p in part], axis=0)

    def heads(start, h):
        raw = query[start : start + TOK, h * HD : (h + 1) * HD]
        turned = raw * cos + pltpu.roll(raw, HD // 2, 1) * sin
        return raw, (turned * scale).astype(jnp.bfloat16)

    keys, values = keys_values(0)
    for h in range(2):
        _, query_head = heads(0, h)
        weights = softmax(matmul(query_head, keys, NN)).astype(jnp.bfloat16)
        attended_ref[:, h * HD : (h + 1) * HD] = matmul(weights, values, NT).astype(jnp.bfloat16)

    keys, values = keys_values(TOK)
    grad_key = jnp.zeros((HD, TOK), jnp.float32)
    grad_value = jnp.zeros((HD, TOK), jnp.float32)
    mixed = jnp.zeros((TOK, HD), jnp.float32)
    for h in range(2):
        raw, query_head = heads(TOK, h)
        probs = softmax(matmul(query_head, keys, NN))
        grad_head = grad_out[:, h * HD : (h + 1) * HD]
        grad_probs = matmul(grad_head, values, NN)
        delta = jnp.sum(probs * grad_probs, axis=-1, keepdims=True)
        grad_scores = (probs * (grad_probs - delta)).astype(jnp.bfloat16)
        turned = matmul(grad_scores, keys, NT)
        grad_query = (turned * cos - pltpu.roll(turned, HD // 2, 1) * sin) * scale
        grad_query = grad_query.astype(jnp.bfloat16)
        grad_query_ref[:, h * HD : (h + 1) * HD] = grad_query
        mixed = mixed + grad_query.astype(jnp.float32) * raw
        grad_key = grad_key + matmul(query_head, grad_scores, TN)
        grad_value = grad_value + matmul(grad_head, probs.astype(jnp.bfloat16), TN)
    cost, sint = table_ref[256:320], table_ref[320:384]
    first, second = grad_key[:64], grad_key[64:]
    key_first = first * cost + second * sint
    key_second = second * cost - first * sint
    for y in range(SIDE):
        grad_kv_ref[y, 0:16] = key_first[16 * y : 16 * y + 16]
        grad_kv_ref[y, 16:32] = key_second[16 * y : 16 * y + 16]
        grad_kv_ref[y, 32:64] = grad_value[32 * y : 32 * y + 32]
    mixed_ref[...] = jnp.broadcast_to(jnp.sum(mixed.T, axis=0, keepdims=True), (8, TOK))


def split_rows(total):
    high = total.astype(jnp.bfloat16)
    low = (total - high.astype(jnp.float32)).astype(jnp.bfloat16)
    row = lax.broadcasted_iota(jnp.int32, (16, TOK), 0)
    both = jnp.where(row == 0, high.astype(jnp.float32), low.astype(jnp.float32))
    both = jnp.where(row < 2, both, 0.0)
    return jnp.concatenate([both, jnp.zeros((16, COLS - TOK), jnp.float32)], axis=1).astype(jnp.bfloat16)


def project(
    attended_ref, grad_query_ref, grad_kv_ref, raw_ref, mixed_ref, qw_ref, ow_ref, rows_ref, out_ref
):
    place = position()
    attended = attended_ref[...]
    grad_query = grad_query_ref[...]
    grad_kv = grad_kv_ref[0] + grad_kv_ref[1] + grad_kv_ref[2] + grad_kv_ref[3]
    grad_kv = grad_kv.astype(jnp.bfloat16)
    mixed = mixed_ref[0:1] + jnp.sum(grad_kv.astype(jnp.float32) * raw_ref[...], axis=0, keepdims=True)
    rows = split_rows(mixed)
    for k in range(SIDE):
        for j in range(SIDE):
            t = block_index(place, k, j)
            block = weight_rows(t)
            start = pl.multiple_of(lax.rem(t, SIDE) * 256, 256)
            term = matmul(attended, ow_ref[:, block], NN)
            out_ref[lax.div(t, SIDE), pl.ds(start, TOK)] = term.astype(jnp.bfloat16)
            term = matmul(grad_query, qw_ref[block, :], NT)
            term = term + matmul(grad_kv, rows_ref[k, 528 + 64 * j : 592 + 64 * j], TN)
            out_ref[lax.div(t, SIDE), pl.ds(start + TOK, TOK)] = term.astype(jnp.bfloat16)
    for x in range(SIDE):
        out_ref[x, 1024:1040] = rows


def sum_first(parts_ref, out_ref):
    rows = jnp.zeros((16, COLS), jnp.float32)
    for k in range(SIDE):
        rows = rows + parts_ref[k, 1024:1040].astype(jnp.float32)
    mixed = split_rows(rows[0:1, :TOK] + rows[1:2, :TOK])
    for j in range(SIDE):
        total = jnp.zeros((256, COLS), jnp.float32)
        for k in range(SIDE):
            total = total + parts_ref[k, j * 256 : j * 256 + 256].astype(jnp.float32)
        out_ref[j, 0:256] = total.astype(jnp.bfloat16)
        out_ref[j, 256:272] = mixed


def finish(parts_ref, rows_ref, back_ref, cot_ref, gain_ref, factor_ref, out_ref, grad_ref):
    total = parts_ref[0].astype(jnp.float32)
    for j in range(1, SIDE):
        total = total + parts_ref[j].astype(jnp.float32)
    out_ref[...] = (rows_ref[...].astype(jnp.float32) + total[0:TOK]).astype(jnp.bfloat16)
    mixed = jnp.broadcast_to(total[256:257, :TOK] + total[257:258, :TOK], (TOK, TOK)).T[:, 0:1]
    factor = factor_ref[:, 0:1]
    scaled = total[TOK : 2 * TOK] * gain_ref[...]
    grad_rows = factor * scaled - back_ref[...].astype(jnp.float32) * (factor * factor * mixed / WIDTH)
    grad_ref[...] = (cot_ref[...].astype(jnp.float32) + grad_rows).astype(jnp.bfloat16)


def per_device(
    section_input,
    stash_pool,
    reload_slot,
    cotangent,
    norm_gain,
    query_weight,
    kv_weight,
    out_weight,
):
    token_rows = section_input[0]
    cot_rows = cotangent[0]
    query_w = query_weight[0]
    kv_w = kv_weight[0]
    out_w = out_weight[0]
    section_count = lax.axis_size("section")
    section_pos = lax.axis_index("section")
    is_early = section_pos < section_count // 2

    picked = lax.dynamic_index_in_dim(stash_pool[0], reload_slot[0], 0, keepdims=False)
    half = section_count // 2
    reloaded = lax.ppermute(picked, "section", [(section_count - 1 - s, s) for s in range(half)])
    cos, sin = rope_angles()
    wide = np.concatenate([cos, cos], axis=1), np.concatenate([-sin, sin], axis=1)
    table = jnp.asarray(np.concatenate([*wide, cos.T, sin.T], axis=0))
    gain_row = norm_gain

    back_rows = call(
        pick_back, (shape((TOK, COLS)),), reloaded, token_rows, flops=2 * 10**10
    )[0]
    held = [pltpu.VMEM(a.shape, a.dtype) for a in (token_rows, gain_row, kv_w)]
    blocks = call(
        first_blocks,
        (shape((SIDE, 400, COLS)),),
        token_rows, gain_row, kv_w,
        scratch=(*held, pltpu.SemaphoreType.DMA((4,))),
        in_place=True,
        vmem=58,
    )[0]
    blocks = exchange(blocks, FIRST)
    blocks = call(second_blocks, (shape((SIDE, 1040, COLS)),), blocks, back_rows, cot_rows)[0]
    rows = exchange(blocks, SECOND)
    evicting, _ = lax.optimization_barrier((token_rows, back_rows))
    evicted = lax.ppermute(evicting, "section", [(s, section_count - 1 - s) for s in range(half)])
    rows, evicted = lax.optimization_barrier((rows, evicted))
    blocks = call(third_blocks, (shape((SIDE, 8 * TOK, COLS)),), rows)[0]
    back = exchange(blocks, FIRST)

    normed, kv_own, kv_raw, factor = call(
        norm_and_kv,
        (
            shape((16, 2 * TOK, COLS)),
            shape((SIDE, 64, 2 * TOK)),
            shape((64, TOK), jnp.float32),
            shape((TOK, HD), jnp.float32),
        ),
        rows, back, table,
        flops=2 * 64 * 256 * 4096,
    )
    kv_all = exchange_row(kv_own, 1)
    attended, grad_query, grad_kv, mixed = call(
        attention,
        (
            shape((TOK, COLS)),
            shape((TOK, COLS)),
            shape((SIDE, 64, TOK), jnp.float32),
            shape((8, TOK), jnp.float32),
        ),
        back, normed, kv_all, query_w, out_w, table,
        flops=2 * 384 * 256 * 4096,
    )
    grad_kv = exchange_row(grad_kv, 1)
    terms = call(
        project,
        (shape((SIDE, 1040, COLS)),),
        attended, grad_query, grad_kv, kv_raw, mixed, query_w, out_w, rows,
        flops=2 * 256 * 256 * 4096,
    )[0]
    terms = exchange_row(terms, 0)
    terms = call(sum_first, (shape((SIDE, 272, COLS)),), terms)[0]
    terms = exchange_row(terms, 1)
    layer_out, grad_local = call(
        finish,
        (shape((TOK, COLS)), shape((TOK, COLS))),
        terms, token_rows, back_rows, cot_rows, gain_row, factor,
    )
    next_input = lax.ppermute(layer_out, "section", [(s, s + 1) for s in range(section_count - 1)])
    input_grad = lax.ppermute(grad_local, "section", [(s + 1, s) for s in range(section_count - 1)])
    next_input, input_grad, received = call(
        deliver, (shape((TOK, COLS)),) * 3, next_input, input_grad, reloaded, evicted
    )
    return (next_input[None], received[None], input_grad[None])


def solution(mesh):
    return jax.shard_map(
        per_device,
        mesh=mesh,
        in_specs=(
            P("section", "dp", "tensor"),
            P("section", None, "dp", "tensor"),
            P("section"),
            P("section", "dp", "tensor"),
            P("section", "tensor"),
            P("section", None, "tensor"),
            P("section", "tensor", None),
            P("section", "tensor", None),
        ),
        out_specs=(
            P("section", "dp", "tensor"),
            P("section", "dp", "tensor"),
            P("section", "dp", "tensor"),
        ),
        check_vma=False,
    )
```
